32 devices in a mesh: wide: 8 (over z, core), narrow: 4 (over y, x).
Axes of the slice: x: 2, y: 2, z: 4, core: 2. Of those that a mesh axis runs over, the one named last changes fastest.
Arguments:
- features: bfloat16 [8192, 128], P(('wide', 'narrow')), may hold values from -6 to 6
- block_values: bfloat16 [4, 8, 96, 128, 128], P('narrow', 'wide'), may hold values from -0.125 to 0.125
- block_rows: int32 [4, 8, 96], P('narrow', 'wide'), may hold values from 0 to 15
- block_cols: int32 [4, 8, 96], P('narrow', 'wide'), may hold values from 0 to 7
- counts: int32 [4, 8], P('narrow', 'wide'), may hold values from 1 to 96, as said below
- weight: bfloat16 [128, 256], replicated, may hold values from -0.5 to 0.5
- bias: float32 [256], replicated, may hold values from -3 to 3
Outputs:
- activations: bfloat16 [8192, 256], P(('narrow', 'wide'))
The draws below stay inside these ranges and needn't reach their ends.
Inputs may be any that keep to these rules, and one draw needn't show every extreme that they name: `counts`: each draw has a tile with all 96 slots used.
All inputs are finite; a program needn't handle non-finite values.
Results may differ from the reference program's by a relative error of at most 0.0046.
Values may be sent and summed in bfloat16 or wider, within the bound.
A program may use at most 64 MiB of HBM per device.

```python
import jax
import jax.numpy as jnp
from jax import lax

F = 128
HID = 256
BLK = 128
ND = 256
KB = 96
NODES = 8192
RBLK = 16
CBLK = 8
N_WIDE = 8
N_NARROW = 4


def draw_counts(key, part):
    first_key, second_key = jax.random.split(jax.random.fold_in(key, 17))
    raw = jax.random.randint(first_key, (N_NARROW * N_WIDE,), 0, KB)
    shaped = 1 + raw * raw // KB
    chosen = jax.random.randint(second_key, (), 0, N_NARROW * N_WIDE)
    filled = jnp.where(jnp.arange(N_NARROW * N_WIDE) == chosen, KB, shaped)
    return filled.reshape(N_NARROW, N_WIDE).astype(jnp.int32)


def plant(values, key, least, high):
    longest = values.shape.index(max(values.shape))
    spots = []
    for shift in (0, 1):
        where = [jax.random.randint(jax.random.fold_in(key, axis), (), 0, length) for axis, length in enumerate(values.shape)]
        where[longest] = (where[longest] + shift) % values.shape[longest]
        spots.append(tuple(where))
    return values.at[spots[0]].set(least).at[spots[1]].set(high)


def levels(rng, dims, cuts, smallest, top_value):
    level = 1.0
    for dim, shards_of in cuts:
        steps = jax.random.uniform(jax.random.fold_in(jax.random.fold_in(rng, 6), dim), (shards_of,), jnp.float32, smallest / len(cuts), top_value / len(cuts))
        level = level * jnp.repeat(jnp.exp(steps), dims[dim] // shards_of).reshape((-1,) + (1,) * (len(dims) - 1 - dim))
    return level


def bell_draw(key, extent, width, reach, shards=(), held_as=jnp.bfloat16):
    factor_of = levels(key, extent, shards, -0.22, 0.18) if shards else 1.0
    values = jax.random.normal(key, extent, jnp.float32) * width * factor_of
    return jnp.minimum(jnp.maximum(values, -reach), reach).astype(held_as)


def setup_inputs(seed: int = 0) -> dict:
    key_list = jax.random.split(jax.random.key(seed), 8)
    features = bell_draw(key_list[0], (NODES, F), 1.0, 6.0, ((0, 32),))
    block_values = bell_draw(key_list[1], (N_NARROW, N_WIDE, KB, BLK, BLK), (BLK * BLK * KB // (3 * ND)) ** -0.5, 0.125, ((0, 4), (1, 8)))
    block_rows = plant(jax.random.randint(key_list[2], (N_NARROW, N_WIDE, KB), 0, RBLK), jax.random.fold_in(key_list[2], 1), 0, RBLK - 1).astype(jnp.int32)
    block_cols = plant(jax.random.randint(key_list[3], (N_NARROW, N_WIDE, KB), 0, CBLK), jax.random.fold_in(key_list[3], 1), 0, CBLK - 1).astype(jnp.int32)
    counts = draw_counts(jax.random.fold_in(key_list[7], 71), 0)
    weight = bell_draw(key_list[5], (F, HID), F ** -0.5, 0.5)
    bias = bell_draw(key_list[6], (HID,), 0.5, 3.0, (), jnp.float32)
    return {"features": features, "block_values": block_values, "block_rows": block_rows, "block_cols": block_cols, "counts": counts, "weight": weight, "bias": bias}


def reference(features, block_values, block_rows, block_cols, counts, weight, bias):
    panel_rows = N_NARROW * ND
    def one_tile(operands):
        values, rows, cols, used, column_panel = operands
        panel_blocks = column_panel.reshape(CBLK, BLK, F)
        picked = panel_blocks[cols.astype(jnp.int32)].astype(jnp.float32)
        products = jnp.einsum("kij,kjf->kif", values.astype(jnp.float32), picked)
        active = (jnp.arange(KB, dtype=jnp.int32) < used).astype(jnp.float32)
        products = products * active[:, None, None]
        summed = jax.ops.segment_sum(products, rows.astype(jnp.int32), num_segments=RBLK)
        return summed.reshape(RBLK * BLK, F)

    def one_panel_row(narrow_index):
        def add_tile(total, wide_index):
            values = block_values[narrow_index, wide_index]
            rows = block_rows[narrow_index, wide_index]
            cols = block_cols[narrow_index, wide_index]
            used = counts[narrow_index, wide_index]
            column_panel = lax.dynamic_slice_in_dim(features, (wide_index * panel_rows).astype(jnp.int32), panel_rows, 0)
            return total + one_tile((values, rows, cols, used, column_panel)), None
        start_total = jnp.zeros((RBLK * BLK, F), jnp.float32)
        total, unused = lax.scan(add_tile, start_total, jnp.arange(N_WIDE, dtype=jnp.int32))
        return total

    aggregated = lax.map(one_panel_row, jnp.arange(N_NARROW, dtype=jnp.int32)).reshape(NODES, F)
    hidden = aggregated.astype(jnp.bfloat16)
    mixed = jnp.dot(hidden, weight, preferred_element_type=jnp.float32) + bias
    return jnp.maximum(mixed, 0.0).astype(jnp.bfloat16)
```

```python
import functools

import jax
import jax.numpy as jnp
from jax import lax
from jax.experimental import pallas as pl
from jax.experimental.pallas import tpu as pltpu
from jax.sharding import PartitionSpec as P

MESH = pl.DeviceIdType.MESH


def bits_for(count):
    return max(1, (count - 1).bit_length())


def group_steps(groups):
    if groups % 2 == 0:
        half = groups // 2
        pairs = [(1, low) for low in range(half)] + [(0, low) for low in range(1, half)] + [(0, 0)]
        return half, pairs
    return groups, [(0, low) for low in range(1, groups)] + [(0, 0)]


def kernel(
    wide_count, narrow_count,
    features, values, rows_in, cols_in, counts, weight, bias,
    out,
    panel, blocks, running, order_v, order_s, pair_out, pair_in, line_out, line_in,
    values_sem, own_sem, order_sem, feat_send, feat_recv, pair_send, pair_recv, line_send, line_recv,
):
    per_device, block, width = features.shape
    slots = blocks.shape[0] - 1
    entries = running.shape[1]
    phases = running.shape[0]
    part = block // phases
    tile_rows = wide_count * per_device
    panel_blocks = narrow_count * per_device
    groups = wide_count // 2
    half, steps = group_steps(groups)
    lanes = order_v.shape[1]
    col_shift = bits_for(lanes)
    row_shift = col_shift + bits_for(panel_blocks)

    wide = lax.axis_index("wide")
    narrow = lax.axis_index("narrow")
    group = lax.div(wide, 2)
    core = lax.rem(wide, 2)
    other = 1 - core
    high, low = lax.div(group, half), lax.rem(group, half)
    targets = [
        lax.rem(high + up, 2) * half + lax.rem(low + along, half) if groups % 2 == 0 else lax.rem(group + along, groups)
        for up, along in steps
    ]
    peers = [lax.rem(narrow + offset, narrow_count) for offset in range(1, narrow_count)]

    chunks = values_sem.shape[0]
    chunk = slots // chunks
    value_copies = [
        pltpu.make_async_copy(
            values.at[0, 0, pl.ds(i * chunk, chunk)], blocks.at[pl.ds(1 + i * chunk, chunk)], values_sem.at[i]
        )
        for i in range(chunks)
    ]
    own_copy = pltpu.make_async_copy(features, panel.at[pl.ds(narrow * per_device, per_device)], own_sem)
    for copy in value_copies:
        copy.start()
    own_copy.start()

    barrier = pltpu.get_barrier_semaphore()
    for peer in peers:
        pl.semaphore_signal(barrier, inc=1, device_id={"narrow": peer}, device_id_type=MESH)
    pl.semaphore_signal(barrier, inc=1, device_id={"wide": group * 2 + other}, device_id_type=MESH)
    for target in targets[:-1]:
        pl.semaphore_signal(barrier, inc=1, device_id={"wide": target * 2 + core}, device_id_type=MESH)

    blocks[0] = jnp.zeros((block, block), blocks.dtype)
    lane = lax.broadcasted_iota(jnp.int32, (1, lanes), 1)
    across = lax.broadcasted_iota(jnp.int32, (lanes, lanes), 1)
    down = lax.broadcasted_iota(jnp.int32, (lanes, lanes), 0)
    order_v[...] = jnp.broadcast_to((tile_rows << row_shift) + lane + 1, order_v.shape)
    slot = lane[:, :slots]
    row = jnp.where(slot < counts[...], rows_in[0], tile_rows)
    order_v[0:1, 0:slots] = (row << row_shift) + (cols_in[0] << col_shift) + slot + 1
    key = order_v[0:1, :]
    key_down = jnp.sum(jnp.where(down == across, key, 0), axis=1, keepdims=True)
    row_down = key_down >> row_shift
    held = jnp.sum((row_down == across).astype(jnp.int32), axis=0, keepdims=True)
    before = (key < key_down).astype(jnp.int32) + jnp.where(across < row_down, held & 1, 0)
    place = jnp.sum(before, axis=1, keepdims=True)
    ordered = jnp.sum(jnp.where((place == across) & (row_down < tile_rows), key_down, 0), axis=0, keepdims=True)
    first = (place & 1) == 0
    upto = jnp.sum(jnp.where((row_down <= across) & first, 1, 0), axis=0, keepdims=True)
    order_v[0:1, :] = ordered & ((1 << col_shift) - 1)
    order_v[1:2, :] = (ordered >> col_shift) & ((1 << (row_shift - col_shift)) - 1)
    order_v[2:3, :] = ordered >> row_shift
    order_v[3:4, :] = jnp.maximum(upto - 1, 0)
    order_v[4:5, :] = held
    order_copy = pltpu.make_async_copy(order_v, order_s, order_sem)
    order_copy.start()

    pl.semaphore_wait(barrier, (narrow_count - 1) + 1 + (groups - 1))

    feature_copies = []
    for i, peer in enumerate(peers):
        copy = pltpu.make_async_remote_copy(
            src_ref=features,
            dst_ref=panel.at[pl.ds(narrow * per_device, per_device)],
            send_sem=feat_send.at[i],
            recv_sem=feat_recv.at[i],
            device_id={"narrow": peer},
            device_id_type=MESH,
        )
        copy.start()
        feature_copies.append(copy)

    for copy in value_copies:
        copy.wait()
    own_copy.wait()
    order_copy.wait()
    for copy in feature_copies:
        copy.wait_recv()

    def sweep(phase, begin, end, total):
        here = pl.ds(phase * part, part)
        unroll = max(u for u in range(1, 9) if (end - begin) % u == 0)

        def some(step, total):
            for j in range(unroll):
                e = begin + step * unroll + j
                keep = jnp.where(order_s[2, 2 * e] == order_s[2, jnp.maximum(2 * e - 2, 0)], 1.0, 0.0)
                left = jnp.concatenate([blocks[order_s[0, 2 * e], here], blocks[order_s[0, 2 * e + 1], here]], axis=1)
                right = jnp.concatenate([panel[order_s[1, 2 * e]], panel[order_s[1, 2 * e + 1]]], axis=0)
                product = jnp.dot(left, right, preferred_element_type=jnp.float32)
                total = total * keep.astype(jnp.float32) + product
                running[phase, e] = total
            return total

        return lax.fori_loop(0, (end - begin) // unroll, some, total)

    def row_sum(phase, r):
        present = jnp.where(order_s[4, r] > 0, 1.0, 0.0).astype(jnp.float32)
        return running[phase, order_s[3, r]] * present

    pair_copies, line_copies, totals = [], [], []

    def send_pair(phase):
        for i, target in enumerate(targets):
            for j in range(per_device):
                pair_out[phase, i, j * part:(j + 1) * part, :] = row_sum(phase, (target * 2 + other) * per_device + j)
            copy = pltpu.make_async_remote_copy(
                src_ref=pair_out.at[phase, i],
                dst_ref=pair_in.at[phase, i],
                send_sem=pair_send.at[phase, i],
                recv_sem=pair_recv.at[phase, i],
                device_id={"wide": group * 2 + other},
                device_id_type=MESH,
            )
            copy.start()
            pair_copies.append(copy)

    def send_line(phase):
        for i, target in enumerate(targets):
            own = jnp.concatenate(
                [row_sum(phase, (target * 2 + core) * per_device + j) for j in range(per_device)], axis=0
            )
            pair_copies[phase * groups + i].wait_recv()
            both = own + pair_in[phase, i]
            if i == groups - 1:
                totals.append(both)
            else:
                line_out[phase, i] = both.astype(jnp.bfloat16)
                copy = pltpu.make_async_remote_copy(
                    src_ref=line_out.at[phase, i],
                    dst_ref=line_in.at[phase, i],
                    send_sem=line_send.at[phase, i],
                    recv_sem=line_recv.at[phase, i],
                    device_id={"wide": target * 2 + core},
                    device_id_type=MESH,
                )
                copy.start()
                line_copies.append(copy)

    middle = entries // 2
    for phase in range(phases):
        total = jnp.zeros((part, width), jnp.float32)
        if phase == 0:
            sweep(phase, 0, entries, total)
        else:
            total = sweep(phase, 0, middle, total)
            send_line(phase - 1)
            sweep(phase, middle, entries, total)
        send_pair(phase)
    send_line(phases - 1)

    for phase in range(phases):
        total = totals[phase]
        for i in range(groups - 1):
            line_copies[phase * (groups - 1) + i].wait_recv()
            total = total + line_in[phase, i].astype(jnp.float32)
        mixed = jnp.dot(total.astype(jnp.bfloat16), weight[...], preferred_element_type=jnp.float32) + bias[...]
        result = jnp.maximum(mixed, 0.0).astype(out.dtype)
        for j in range(per_device):
            out[pl.ds(j * block + phase * part, part), :] = result[j * part:(j + 1) * part]

    for copy in feature_copies + pair_copies + line_copies:
        copy.wait_send()


def shards(features, block_values, block_rows, block_cols, counts, weight, bias):
    wide_count = lax.axis_size("wide")
    narrow_count = lax.axis_size("narrow")
    nodes, width = features.shape
    slots, block = block_values.shape[2], block_values.shape[3]
    per_device = nodes // block
    groups = wide_count // 2
    hidden = weight.shape[1]
    tile_rows = wide_count * per_device
    entries = (slots + min(slots, tile_rows)) // 2
    lanes = -(-(slots + tile_rows) // 128) * 128
    phases = 2
    part_nodes = nodes // phases
    others_in_line = max(groups - 1, 1)
    chunks = max(c for c in (1, 2, 4) if slots % c == 0)
    others = max(narrow_count - 1, 1)
    in_vmem = pl.BlockSpec(memory_space=pltpu.VMEM)
    in_hbm = pl.BlockSpec(memory_space=pltpu.HBM)
    dma = pltpu.SemaphoreType.DMA
    return pl.pallas_call(
        functools.partial(kernel, wide_count, narrow_count),
        out_shape=jax.ShapeDtypeStruct((nodes, hidden), jnp.bfloat16),
        in_specs=[in_hbm, in_hbm] + [in_vmem] * 5,
        out_specs=in_vmem,
        scratch_shapes=[
            pltpu.VMEM((narrow_count * per_device, block, width), jnp.bfloat16),
            pltpu.VMEM((slots + 1, block, block), jnp.bfloat16),
            pltpu.VMEM((phases, entries, block // phases, width), jnp.float32),
            pltpu.VMEM((8, lanes), jnp.int32),
            pltpu.SMEM((8, lanes), jnp.int32),
            pltpu.VMEM((phases, groups, part_nodes, width), jnp.float32),
            pltpu.VMEM((phases, groups, part_nodes, width), jnp.float32),
            pltpu.VMEM((phases, others_in_line, part_nodes, width), jnp.bfloat16),
            pltpu.VMEM((phases, others_in_line, part_nodes, width), jnp.bfloat16),
            dma((chunks,)),
            dma,
            dma,
            dma((others,)),
            dma((others,)),
            dma((phases, groups)),
            dma((phases, groups)),
            dma((phases, others_in_line)),
            dma((phases, others_in_line)),
        ],
        compiler_params=pltpu.CompilerParams(
            collective_id=0, has_side_effects=True, vmem_limit_bytes=56 * 1024 * 1024
        ),
        cost_estimate=pl.CostEstimate(
            flops=2 * slots * block * block * width, bytes_accessed=2 * slots * block * block, transcendentals=0
        ),
    )(
        features.reshape(per_device, block, width), block_values, block_rows, block_cols, counts,
        weight, bias.reshape(1, hidden),
    )


def solution(mesh):
    placed = (
        P(("wide", "narrow"), None),
        P("narrow", "wide", None, None, None),
        P("narrow", "wide", None),
        P("narrow", "wide", None),
        P("narrow", "wide"),
        P(),
        P(),
    )
    return jax.shard_map(
        shards, mesh=mesh, in_specs=placed, out_specs=P(("narrow", "wide"), None), check_vma=False
    )
```

```python
import functools

import jax
import jax.numpy as jnp
from jax import lax
from jax.experimental import pallas as pl
from jax.experimental.pallas import tpu as pltpu
from jax.sharding import PartitionSpec as P

MESH = pl.DeviceIdType.MESH


def bits_for(count):
    return max(1, (count - 1).bit_length())


def group_steps(groups):
    if groups % 2 == 0:
        half = groups // 2
        pairs = [(1, low) for low in range(half)] + [(0, low) for low in range(1, half)] + [(0, 0)]
        return half, pairs
    return groups, [(0, low) for low in range(1, groups)] + [(0, 0)]


def kernel(
    wide_count, narrow_count,
    features, values, rows_in, cols_in, counts, weight, bias,
    out,
    panel, blocks, running, order_v, order_s, pair_out, pair_in, line_out, line_in,
    values_sem, own_sem, order_sem, feat_send, feat_recv, pair_send, pair_recv, line_send, line_recv,
):
    per_device, block, width = features.shape
    slots = blocks.shape[0] - 1
    entries = running.shape[1]
    phases = running.shape[0]
    part = block // phases
    tile_rows = wide_count * per_device
    panel_blocks = narrow_count * per_device
    groups = wide_count // 2
    half, steps = group_steps(groups)
    lanes = order_v.shape[1]
    col_shift = bits_for(lanes)
    row_shift = col_shift + bits_for(panel_blocks)

    wide = lax.axis_index("wide")
    narrow = lax.axis_index("narrow")
    group = lax.div(wide, 2)
    core = lax.rem(wide, 2)
    other = 1 - core
    high, low = lax.div(group, half), lax.rem(group, half)
    targets = [
        lax.rem(high + up, 2) * half + lax.rem(low + along, half) if groups % 2 == 0 else lax.rem(group + along, groups)
        for up, along in steps
    ]
    peers = [lax.rem(narrow + offset, narrow_count) for offset in range(1, narrow_count)]

    chunks = values_sem.shape[0]
    chunk = slots // chunks
    value_copies = [
        pltpu.make_async_copy(
            values.at[0, 0, pl.ds(i * chunk, chunk)], blocks.at[pl.ds(1 + i * chunk, chunk)], values_sem.at[i]
        )
        for i in range(chunks)
    ]
    own_copy = pltpu.make_async_copy(features, panel.at[pl.ds(narrow * per_device, per_device)], own_sem)
    for copy in value_copies:
        copy.start()
    own_copy.start()

    barrier = pltpu.get_barrier_semaphore()
    for peer in peers:
        pl.semaphore_signal(barrier, inc=1, device_id={"narrow": peer}, device_id_type=MESH)
    pl.semaphore_signal(barrier, inc=1, device_id={"wide": group * 2 + other}, device_id_type=MESH)
    for target in targets[:-1]:
        pl.semaphore_signal(barrier, inc=1, device_id={"wide": target * 2 + core}, device_id_type=MESH)

    blocks[0] = jnp.zeros((block, block), blocks.dtype)
    lane = lax.broadcasted_iota(jnp.int32, (1, lanes), 1)
    across = lax.broadcasted_iota(jnp.int32, (lanes, lanes), 1)
    down = lax.broadcasted_iota(jnp.int32, (lanes, lanes), 0)
    order_v[...] = jnp.broadcast_to((tile_rows << row_shift) + lane + 1, order_v.shape)
    slot = lane[:, :slots]
    row = jnp.where(slot < counts[...], rows_in[0], tile_rows)
    order_v[0:1, 0:slots] = (row << row_shift) + (cols_in[0] << col_shift) + slot + 1
    key = order_v[0:1, :]
    key_down = jnp.sum(jnp.where(down == across, key, 0), axis=1, keepdims=True)
    row_down = key_down >> row_shift
    held = jnp.sum((row_down == across).astype(jnp.int32), axis=0, keepdims=True)
    before = (key < key_down).astype(jnp.int32) + jnp.where(across < row_down, held & 1, 0)
    place = jnp.sum(before, axis=1, keepdims=True)
    ordered = jnp.sum(jnp.where((place == across) & (row_down < tile_rows), key_down, 0), axis=0, keepdims=True)
    first = (place & 1) == 0
    upto = jnp.sum(jnp.where((row_down <= across) & first, 1, 0), axis=0, keepdims=True)
    order_v[0:1, :] = ordered & ((1 << col_shift) - 1)
    order_v[1:2, :] = (ordered >> col_shift) & ((1 << (row_shift - col_shift)) - 1)
    order_v[2:3, :] = ordered >> row_shift
    order_v[3:4, :] = jnp.maximum(upto - 1, 0)
    order_v[4:5, :] = held
    order_copy = pltpu.make_async_copy(order_v, order_s, order_sem)
    order_copy.start()

    pl.semaphore_wait(barrier, (narrow_count - 1) + 1 + (groups - 1))

    feature_copies = []
    for i, peer in enumerate(peers):
        copy = pltpu.make_async_remote_copy(
            src_ref=features,
            dst_ref=panel.at[pl.ds(narrow * per_device, per_device)],
            send_sem=feat_send.at[i],
            recv_sem=feat_recv.at[i],
            device_id={"narrow": peer},
            device_id_type=MESH,
        )
        copy.start()
        feature_copies.append(copy)

    for copy in value_copies:
        copy.wait()
    own_copy.wait()
    order_copy.wait()
    for copy in feature_copies:
        copy.wait_recv()

    def sweep(phase, begin, end, total):
        here = pl.ds(phase * part, part)
        unroll = max(u for u in range(1, 9) if (end - begin) % u == 0)

        def some(step, total):
            products, keeps = [], []
            for j in range(unroll):
                e = begin + step * unroll + j
                keep = jnp.where(order_s[2, 2 * e] == order_s[2, jnp.maximum(2 * e - 2, 0)], 1.0, 0.0)
                keeps.append(keep.astype(jnp.float32))
                left = jnp.concatenate([blocks[order_s[0, 2 * e], here], blocks[order_s[0, 2 * e + 1], here]], axis=1)
                right = jnp.concatenate([panel[order_s[1, 2 * e]], panel[order_s[1, 2 * e + 1]]], axis=0)
                products.append(jnp.dot(left, right, preferred_element_type=jnp.float32))
            for j in range(unroll):
                total = total * keeps[j] + products[j]
                running[phase, begin + step * unroll + j] = total
            return total

        return lax.fori_loop(0, (end - begin) // unroll, some, total)

    def row_sum(phase, r):
        present = jnp.where(order_s[4, r] > 0, 1.0, 0.0).astype(jnp.float32)
        return running[phase, order_s[3, r]] * present

    pair_copies, line_copies, totals = [], [], []

    def send_pair(phase):
        for i, target in enumerate(targets):
            for j in range(per_device):
                pair_out[phase, i, j * part:(j + 1) * part, :] = row_sum(phase, (target * 2 + other) * per_device + j)
            copy = pltpu.make_async_remote_copy(
                src_ref=pair_out.at[phase, i],
                dst_ref=pair_in.at[phase, i],
                send_sem=pair_send.at[phase, i],
                recv_sem=pair_recv.at[phase, i],
                device_id={"wide": group * 2 + other},
                device_id_type=MESH,
            )
            copy.start()
            pair_copies.append(copy)

    def send_line(phase):
        for i, target in enumerate(targets):
            own = jnp.concatenate(
                [row_sum(phase, (target * 2 + core) * per_device + j) for j in range(per_device)], axis=0
            )
            pair_copies[phase * groups + i].wait_recv()
            both = own + pair_in[phase, i]
            if i == groups - 1:
                totals.append(both)
            else:
                line_out[phase, i] = both.astype(jnp.bfloat16)
                copy = pltpu.make_async_remote_copy(
                    src_ref=line_out.at[phase, i],
                    dst_ref=line_in.at[phase, i],
                    send_sem=line_send.at[phase, i],
                    recv_sem=line_recv.at[phase, i],
                    device_id={"wide": target * 2 + core},
                    device_id_type=MESH,
                )
                copy.start()
                line_copies.append(copy)

    middle = entries // 2
    for phase in range(phases):
        total = jnp.zeros((part, width), jnp.float32)
        if phase == 0:
            sweep(phase, 0, entries, total)
        else:
            total = sweep(phase, 0, middle, total)
            send_line(phase - 1)
            sweep(phase, middle, entries, total)
        send_pair(phase)
    send_line(phases - 1)

    for phase in range(phases):
        total = totals[phase]
        for i in range(groups - 1):
            line_copies[phase * (groups - 1) + i].wait_recv()
            total = total + line_in[phase, i].astype(jnp.float32)
        mixed = jnp.dot(total.astype(jnp.bfloat16), weight[...], preferred_element_type=jnp.float32) + bias[...]
        result = jnp.maximum(mixed, 0.0).astype(out.dtype)
        for j in range(per_device):
            out[pl.ds(j * block + phase * part, part), :] = result[j * part:(j + 1) * part]

    for copy in feature_copies + pair_copies + line_copies:
        copy.wait_send()


def shards(features, block_values, block_rows, block_cols, counts, weight, bias):
    wide_count = lax.axis_size("wide")
    narrow_count = lax.axis_size("narrow")
    nodes, width = features.shape
    slots, block = block_values.shape[2], block_values.shape[3]
    per_device = nodes // block
    groups = wide_count // 2
    hidden = weight.shape[1]
    tile_rows = wide_count * per_device
    entries = (slots + min(slots, tile_rows)) // 2
    lanes = -(-(slots + tile_rows) // 128) * 128
    phases = 2
    part_nodes = nodes // phases
    others_in_line = max(groups - 1, 1)
    chunks = max(c for c in (1, 2, 4) if slots % c == 0)
    others = max(narrow_count - 1, 1)
    in_vmem = pl.BlockSpec(memory_space=pltpu.VMEM)
    in_hbm = pl.BlockSpec(memory_space=pltpu.HBM)
    dma = pltpu.SemaphoreType.DMA
    return pl.pallas_call(
        functools.partial(kernel, wide_count, narrow_count),
        out_shape=jax.ShapeDtypeStruct((nodes, hidden), jnp.bfloat16),
        in_specs=[in_hbm, in_hbm] + [in_vmem] * 5,
        out_specs=in_vmem,
        scratch_shapes=[
            pltpu.VMEM((narrow_count * per_device, block, width), jnp.bfloat16),
            pltpu.VMEM((slots + 1, block, block), jnp.bfloat16),
            pltpu.VMEM((phases, entries, block // phases, width), jnp.float32),
            pltpu.VMEM((8, lanes), jnp.int32),
            pltpu.SMEM((8, lanes), jnp.int32),
            pltpu.VMEM((phases, groups, part_nodes, width), jnp.float32),
            pltpu.VMEM((phases, groups, part_nodes, width), jnp.float32),
            pltpu.VMEM((phases, others_in_line, part_nodes, width), jnp.bfloat16),
            pltpu.VMEM((phases, others_in_line, part_nodes, width), jnp.bfloat16),
            dma((chunks,)),
            dma,
            dma,
            dma((others,)),
            dma((others,)),
            dma((phases, groups)),
            dma((phases, groups)),
            dma((phases, others_in_line)),
            dma((phases, others_in_line)),
        ],
        compiler_params=pltpu.CompilerParams(
            collective_id=0, has_side_effects=True, vmem_limit_bytes=56 * 1024 * 1024
        ),
        cost_estimate=pl.CostEstimate(
            flops=2 * slots * block * block * width, bytes_accessed=2 * slots * block * block, transcendentals=0
        ),
    )(
        features.reshape(per_device, block, width), block_values, block_rows, block_cols, counts,
        weight, bias.reshape(1, hidden),
    )


def solution(mesh):
    placed = (
        P(("wide", "narrow"), None),
        P("narrow", "wide", None, None, None),
        P("narrow", "wide", None),
        P("narrow", "wide", None),
        P("narrow", "wide"),
        P(),
        P(),
    )
    return jax.shard_map(
        shards, mesh=mesh, in_specs=placed, out_specs=P(("narrow", "wide"), None), check_vma=False
    )
```

```python
import functools

import jax
import jax.numpy as jnp
from jax import lax
from jax.experimental import pallas as pl
from jax.experimental.pallas import tpu as pltpu
from jax.sharding import PartitionSpec as P

MESH = pl.DeviceIdType.MESH


def bits_for(count):
    return max(1, (count - 1).bit_length())


def group_steps(groups):
    if groups % 2 == 0:
        half = groups // 2
        pairs = [(1, low) for low in range(half)] + [(0, low) for low in range(1, half)] + [(0, 0)]
        return half, pairs
    return groups, [(0, low) for low in range(1, groups)] + [(0, 0)]


def slot_kernel(
    wide_count, narrow_count,
    features, values, rows_in, cols_in, counts, weight, bias,
    out,
    panel, blocks, running, order_v, order_s, pair_out, pair_in, line_out, line_in,
    values_sem, own_sem, order_sem, feat_send, feat_recv, pair_send, pair_recv, line_send, line_recv,
):
    per_device, block, width = features.shape
    slots = blocks.shape[0]
    tile_rows = wide_count * per_device
    panel_blocks = narrow_count * per_device
    groups = wide_count // 2
    half, steps = group_steps(groups)
    lanes = order_v.shape[1]
    col_shift = bits_for(lanes)
    row_shift = col_shift + bits_for(panel_blocks)

    wide = lax.axis_index("wide")
    narrow = lax.axis_index("narrow")
    group = lax.div(wide, 2)
    core = lax.rem(wide, 2)
    other = 1 - core
    high, low = lax.div(group, half), lax.rem(group, half)
    targets = [
        lax.rem(high + up, 2) * half + lax.rem(low + along, half) if groups % 2 == 0 else lax.rem(group + along, groups)
        for up, along in steps
    ]
    peers = [lax.rem(narrow + offset, narrow_count) for offset in range(1, narrow_count)]

    chunks = values_sem.shape[0]
    chunk = slots // chunks
    value_copies = [
        pltpu.make_async_copy(
            values.at[0, 0, pl.ds(i * chunk, chunk)], blocks.at[pl.ds(i * chunk, chunk)], values_sem.at[i]
        )
        for i in range(chunks)
    ]
    own_copy = pltpu.make_async_copy(features, panel.at[pl.ds(narrow * per_device, per_device)], own_sem)
    for copy in value_copies:
        copy.start()
    own_copy.start()

    barrier = pltpu.get_barrier_semaphore()
    for peer in peers:
        pl.semaphore_signal(barrier, inc=1, device_id={"narrow": peer}, device_id_type=MESH)
    pl.semaphore_signal(barrier, inc=1, device_id={"wide": group * 2 + other}, device_id_type=MESH)
    for target in targets[:-1]:
        pl.semaphore_signal(barrier, inc=1, device_id={"wide": target * 2 + core}, device_id_type=MESH)

    lane = lax.broadcasted_iota(jnp.int32, (1, lanes), 1)
    across = lax.broadcasted_iota(jnp.int32, (lanes, lanes), 1)
    down = lax.broadcasted_iota(jnp.int32, (lanes, lanes), 0)
    order_v[...] = jnp.broadcast_to((tile_rows << row_shift) + lane, order_v.shape)
    slot = lane[:, :slots]
    row = jnp.where(slot < counts[...], rows_in[0], tile_rows)
    order_v[0:1, 0:slots] = (row << row_shift) + (cols_in[0] << col_shift) + slot
    key = order_v[0:1, :]
    key_down = jnp.sum(jnp.where(down == across, key, 0), axis=1, keepdims=True)
    rank = jnp.sum((key < key_down).astype(jnp.int32), axis=1, keepdims=True)
    ordered = jnp.sum(jnp.where(rank == across, key_down, 0), axis=0, keepdims=True)
    row_down = key_down >> row_shift
    upto = jnp.sum((row_down <= across).astype(jnp.int32), axis=0, keepdims=True)
    held = jnp.sum((row_down == across).astype(jnp.int32), axis=0, keepdims=True)
    order_v[0:1, :] = ordered & ((1 << col_shift) - 1)
    order_v[1:2, :] = (ordered >> col_shift) & ((1 << (row_shift - col_shift)) - 1)
    order_v[2:3, :] = ordered >> row_shift
    order_v[3:4, :] = jnp.maximum(upto - 1, 0)
    order_v[4:5, :] = held
    order_copy = pltpu.make_async_copy(order_v, order_s, order_sem)
    order_copy.start()

    pl.semaphore_wait(barrier, (narrow_count - 1) + 1 + (groups - 1))

    feature_copies = []
    for i, peer in enumerate(peers):
        copy = pltpu.make_async_remote_copy(
            src_ref=features,
            dst_ref=panel.at[pl.ds(narrow * per_device, per_device)],
            send_sem=feat_send.at[i],
            recv_sem=feat_recv.at[i],
            device_id={"narrow": peer},
            device_id_type=MESH,
        )
        copy.start()
        feature_copies.append(copy)

    for copy in value_copies:
        copy.wait()
    own_copy.wait()
    order_copy.wait()
    for copy in feature_copies:
        copy.wait_recv()

    unroll = max(u for u in range(1, 9) if slots % u == 0)

    def sweep(step, total):
        for j in range(unroll):
            p = step * unroll + j
            before = jnp.maximum(p - 1, 0)
            keep = jnp.where(order_s[2, p] == order_s[2, before], 1.0, 0.0).astype(jnp.float32)
            product = jnp.dot(blocks[order_s[0, p]], panel[order_s[1, p]], preferred_element_type=jnp.float32)
            total = total * keep + product
            running[p] = total
        return total

    lax.fori_loop(0, slots // unroll, sweep, jnp.zeros((block, width), jnp.float32))

    def row_sum(r):
        present = jnp.where(order_s[4, r] > 0, 1.0, 0.0).astype(jnp.float32)
        return running[order_s[3, r]] * present

    pair_copies = []
    for i, target in enumerate(targets):
        for j in range(per_device):
            pair_out[i, j * block:(j + 1) * block, :] = row_sum((target * 2 + other) * per_device + j)
        copy = pltpu.make_async_remote_copy(
            src_ref=pair_out.at[i],
            dst_ref=pair_in.at[i],
            send_sem=pair_send.at[i],
            recv_sem=pair_recv.at[i],
            device_id={"wide": group * 2 + other},
            device_id_type=MESH,
        )
        copy.start()
        pair_copies.append(copy)

    line_copies = []
    total = None
    for i, target in enumerate(targets):
        own = jnp.concatenate(
            [row_sum((target * 2 + core) * per_device + j) for j in range(per_device)], axis=0
        )
        pair_copies[i].wait_recv()
        both = own + pair_in[i]
        if i == groups - 1:
            total = both
        else:
            line_out[i] = both.astype(jnp.bfloat16)
            copy = pltpu.make_async_remote_copy(
                src_ref=line_out.at[i],
                dst_ref=line_in.at[i],
                send_sem=line_send.at[i],
                recv_sem=line_recv.at[i],
                device_id={"wide": target * 2 + core},
                device_id_type=MESH,
            )
            copy.start()
            line_copies.append(copy)

    for i, copy in enumerate(line_copies):
        copy.wait_recv()
        total = total + line_in[i].astype(jnp.float32)
    mixed = jnp.dot(total.astype(jnp.bfloat16), weight[...], preferred_element_type=jnp.float32) + bias[...]
    out[...] = jnp.maximum(mixed, 0.0).astype(out.dtype)

    for copy in feature_copies + pair_copies + line_copies:
        copy.wait_send()


def dense_kernel(
    wide_count, narrow_count,
    features, values, rows_in, cols_in, counts, weight, bias,
    out,
    panel, blocks, running, dense, sums, order_v, order_s, pair_out, pair_in, line_out, line_in,
    values_sem, own_sem, order_sem, feat_send, feat_recv, pair_send, pair_recv, line_send, line_recv,
):
    nodes, width = features.shape
    slots, block = blocks.shape[0], blocks.shape[1]
    per_device = nodes // block
    tile_rows = wide_count * per_device
    panel_blocks = narrow_count * per_device
    spots = tile_rows * panel_blocks
    groups = wide_count // 2
    half, steps = group_steps(groups)
    lanes = order_v.shape[1]
    shift = bits_for(lanes)

    wide = lax.axis_index("wide")
    narrow = lax.axis_index("narrow")
    group = lax.div(wide, 2)
    core = lax.rem(wide, 2)
    other = 1 - core
    high, low = lax.div(group, half), lax.rem(group, half)
    targets = [
        lax.rem(high + up, 2) * half + lax.rem(low + along, half) if groups % 2 == 0 else lax.rem(group + along, groups)
        for up, along in steps
    ]
    peers = [lax.rem(narrow + offset, narrow_count) for offset in range(1, narrow_count)]

    chunks = values_sem.shape[0]
    chunk = slots // chunks
    value_copies = [
        pltpu.make_async_copy(
            values.at[0, 0, pl.ds(i * chunk, chunk)], blocks.at[pl.ds(i * chunk, chunk)], values_sem.at[i]
        )
        for i in range(chunks)
    ]
    own_copy = pltpu.make_async_copy(features, panel.at[narrow], own_sem)
    for copy in value_copies:
        copy.start()
    own_copy.start()

    barrier = pltpu.get_barrier_semaphore()
    for peer in peers:
        pl.semaphore_signal(barrier, inc=1, device_id={"narrow": peer}, device_id_type=MESH)
    pl.semaphore_signal(barrier, inc=1, device_id={"wide": group * 2 + other}, device_id_type=MESH)
    for target in targets[:-1]:
        pl.semaphore_signal(barrier, inc=1, device_id={"wide": target * 2 + core}, device_id_type=MESH)

    lane = lax.broadcasted_iota(jnp.int32, (1, lanes), 1)
    across = lax.broadcasted_iota(jnp.int32, (lanes, lanes), 1)
    down = lax.broadcasted_iota(jnp.int32, (lanes, lanes), 0)
    order_v[...] = jnp.broadcast_to((spots << shift) + lane, order_v.shape)
    slot = lane[:, :slots]
    spot = jnp.where(slot < counts[...], rows_in[0] * panel_blocks + cols_in[0], spots)
    order_v[0:1, 0:slots] = (spot << shift) + slot
    key = order_v[0:1, :]
    key_down = jnp.sum(jnp.where(down == across, key, 0), axis=1, keepdims=True)
    rank = jnp.sum((key < key_down).astype(jnp.int32), axis=1, keepdims=True)
    ordered = jnp.sum(jnp.where(rank == across, key_down, 0), axis=0, keepdims=True)
    spot_down = key_down >> shift
    upto = jnp.sum((spot_down <= across).astype(jnp.int32), axis=0, keepdims=True)
    held = jnp.sum((spot_down == across).astype(jnp.int32), axis=0, keepdims=True)
    order_v[0:1, :] = ordered & ((1 << shift) - 1)
    order_v[1:2, :] = ordered >> shift
    order_v[2:3, :] = jnp.where(held > 0, upto, 0)
    order_copy = pltpu.make_async_copy(order_v, order_s, order_sem)
    order_copy.start()

    pl.semaphore_wait(barrier, (narrow_count - 1) + 1 + (groups - 1))

    feature_copies = []
    for i, peer in enumerate(peers):
        copy = pltpu.make_async_remote_copy(
            src_ref=features,
            dst_ref=panel.at[narrow],
            send_sem=feat_send.at[i],
            recv_sem=feat_recv.at[i],
            device_id={"narrow": peer},
            device_id_type=MESH,
        )
        copy.start()
        feature_copies.append(copy)

    running[0] = jnp.zeros((block, block), running.dtype)
    order_copy.wait()
    for copy in value_copies:
        copy.wait()
    unroll = max(u for u in range(1, 9) if slots % u == 0)

    def sweep(step, total):
        for j in range(unroll):
            p = step * unroll + j
            keep = jnp.where(order_s[1, p] == order_s[1, jnp.maximum(p - 1, 0)], 1.0, 0.0)
            total = total * keep.astype(jnp.float32) + blocks[order_s[0, p]].astype(jnp.float32)
            running[p + 1] = total.astype(running.dtype)
        return total

    lax.fori_loop(0, slots // unroll, sweep, jnp.zeros((block, block), jnp.float32))

    def place(r, carry):
        for c in range(panel_blocks):
            dense[c // per_device, pl.ds(pl.multiple_of(r * block, block), block),
                  (c % per_device) * block:(c % per_device + 1) * block] = running[order_s[2, r * panel_blocks + c]]
        return carry

    lax.fori_loop(0, tile_rows, place, 0)

    own_copy.wait()
    sources = [narrow] + [lax.rem(narrow + narrow_count - offset, narrow_count) for offset in range(1, narrow_count)]
    turns = [0] + list(range(1, narrow_count - 1, 2)) + list(range(narrow_count - 1, 0, -2))
    turns = list(dict.fromkeys(turns + list(range(narrow_count))))
    for n, turn in enumerate(turns[:-1]):
        if turn:
            feature_copies[turn - 1].wait_recv()
        source = sources[turn]

        def multiply(d, carry):
            here = pl.ds(pl.multiple_of(d * nodes, nodes), nodes)
            product = jnp.dot(dense[source, here], panel[source], preferred_element_type=jnp.float32)
            sums[here] = product if n == 0 else sums[here] + product
            return carry

        lax.fori_loop(0, wide_count, multiply, 0, unroll=True)
    if turns[-1]:
        feature_copies[turns[-1] - 1].wait_recv()
    final = sources[turns[-1]]

    def chunk_sum(d):
        here = pl.ds(pl.multiple_of(d * nodes, nodes), nodes)
        product = jnp.dot(dense[final, here], panel[final], preferred_element_type=jnp.float32)
        return product + sums[here] if narrow_count > 1 else product

    pair_copies = []
    for i, target in enumerate(targets):
        pair_out[i] = chunk_sum(target * 2 + other)
        copy = pltpu.make_async_remote_copy(
            src_ref=pair_out.at[i],
            dst_ref=pair_in.at[i],
            send_sem=pair_send.at[i],
            recv_sem=pair_recv.at[i],
            device_id={"wide": group * 2 + other},
            device_id_type=MESH,
        )
        copy.start()
        pair_copies.append(copy)

    line_copies = []
    total = None
    for i, target in enumerate(targets):
        own = chunk_sum(target * 2 + core)
        pair_copies[i].wait_recv()
        both = own + pair_in[i]
        if i == groups - 1:
            total = both
        else:
            line_out[i] = both.astype(jnp.bfloat16)
            copy = pltpu.make_async_remote_copy(
                src_ref=line_out.at[i],
                dst_ref=line_in.at[i],
                send_sem=line_send.at[i],
                recv_sem=line_recv.at[i],
                device_id={"wide": target * 2 + core},
                device_id_type=MESH,
            )
            copy.start()
            line_copies.append(copy)

    for i, copy in enumerate(line_copies):
        copy.wait_recv()
        total = total + line_in[i].astype(jnp.float32)
    mixed = jnp.dot(total.astype(jnp.bfloat16), weight[...], preferred_element_type=jnp.float32) + bias[...]
    out[...] = jnp.maximum(mixed, 0.0).astype(out.dtype)

    for copy in feature_copies + pair_copies + line_copies:
        copy.wait_send()


DENSE_BYTES = 8 * 1024 * 1024


def shards(features, block_values, block_rows, block_cols, counts, weight, bias):
    wide_count = lax.axis_size("wide")
    narrow_count = lax.axis_size("narrow")
    nodes, width = features.shape
    slots, block = block_values.shape[2], block_values.shape[3]
    per_device = nodes // block
    groups = wide_count // 2
    hidden = weight.shape[1]
    tile_rows = wide_count * per_device
    panel_blocks = narrow_count * per_device
    dense_fits = tile_rows * panel_blocks * block * block * 2 <= DENSE_BYTES
    keys = tile_rows * panel_blocks if dense_fits else tile_rows
    lanes = -(-max(slots, keys) // 128) * 128
    chunks = max(c for c in (1, 2, 4) if slots % c == 0)
    others = max(narrow_count - 1, 1)
    in_vmem = pl.BlockSpec(memory_space=pltpu.VMEM)
    in_hbm = pl.BlockSpec(memory_space=pltpu.HBM)
    dma = pltpu.SemaphoreType.DMA
    return pl.pallas_call(
        functools.partial(dense_kernel if dense_fits else slot_kernel, wide_count, narrow_count),
        out_shape=jax.ShapeDtypeStruct((nodes, hidden), jnp.bfloat16),
        in_specs=[in_hbm, in_hbm] + [in_vmem] * 5,
        out_specs=in_vmem,
        scratch_shapes=[
            *(
                [
                    pltpu.VMEM((narrow_count, nodes, width), jnp.bfloat16),
                    pltpu.VMEM((slots, block, block), jnp.bfloat16),
                    pltpu.VMEM((slots + 1, block, block), jnp.bfloat16),
                    pltpu.VMEM((narrow_count, wide_count * nodes, nodes), jnp.bfloat16),
                    pltpu.VMEM((wide_count * nodes, width), jnp.float32),
                ]
                if dense_fits
                else [
                    pltpu.VMEM((panel_blocks, block, width), jnp.bfloat16),
                    pltpu.VMEM((slots, block, block), jnp.bfloat16),
                    pltpu.VMEM((slots, block, width), jnp.float32),
                ]
            ),
            pltpu.VMEM((8, lanes), jnp.int32),
            pltpu.SMEM((8, lanes), jnp.int32),
            pltpu.VMEM((groups, nodes, width), jnp.float32),
            pltpu.VMEM((groups, nodes, width), jnp.float32),
            pltpu.VMEM((max(groups - 1, 1), nodes, width), jnp.bfloat16),
            pltpu.VMEM((max(groups - 1, 1), nodes, width), jnp.bfloat16),
            dma((chunks,)),
            dma,
            dma,
            dma((others,)),
            dma((others,)),
            dma((groups,)),
            dma((groups,)),
            dma((max(groups - 1, 1),)),
            dma((max(groups - 1, 1),)),
        ],
        compiler_params=pltpu.CompilerParams(
            collective_id=0 if dense_fits else 1, has_side_effects=True, vmem_limit_bytes=56 * 1024 * 1024
        ),
        cost_estimate=pl.CostEstimate(
            flops=2 * slots * block * block * width, bytes_accessed=2 * slots * block * block, transcendentals=0
        ),
    )(
        features if dense_fits else features.reshape(per_device, block, width), block_values, block_rows, block_cols, counts,
        weight, bias.reshape(1, hidden),
    )


def solution(mesh):
    placed = (
        P(("wide", "narrow"), None),
        P("narrow", "wide", None, None, None),
        P("narrow", "wide", None),
        P("narrow", "wide", None),
        P("narrow", "wide"),
        P(),
        P(),
    )
    return jax.shard_map(
        shards, mesh=mesh, in_specs=placed, out_specs=P(("narrow", "wide"), None), check_vma=False
    )
```

```python
import functools

import jax
import jax.numpy as jnp
from jax import lax
from jax.experimental import pallas as pl
from jax.experimental.pallas import tpu as pltpu
from jax.sharding import PartitionSpec as P

MESH = pl.DeviceIdType.MESH


def bits_for(count):
    return max(1, (count - 1).bit_length())


def group_steps(groups):
    if groups % 2 == 0:
        half = groups // 2
        pairs = [(1, low) for low in range(half)] + [(0, low) for low in range(1, half)] + [(0, 0)]
        return half, pairs
    return groups, [(0, low) for low in range(1, groups)] + [(0, 0)]


def slot_kernel(
    wide_count, narrow_count,
    features, values, rows_in, cols_in, counts, weight, bias,
    out,
    panel, blocks, running, order_v, order_s, pair_out, pair_in, line_out, line_in,
    values_sem, own_sem, order_sem, feat_send, feat_recv, pair_send, pair_recv, line_send, line_recv,
):
    per_device, block, width = features.shape
    slots = blocks.shape[0]
    tile_rows = wide_count * per_device
    panel_blocks = narrow_count * per_device
    groups = wide_count // 2
    half, steps = group_steps(groups)
    lanes = order_v.shape[1]
    col_shift = bits_for(lanes)
    row_shift = col_shift + bits_for(panel_blocks)

    wide = lax.axis_index("wide")
    narrow = lax.axis_index("narrow")
    group = lax.div(wide, 2)
    core = lax.rem(wide, 2)
    other = 1 - core
    high, low = lax.div(group, half), lax.rem(group, half)
    targets = [
        lax.rem(high + up, 2) * half + lax.rem(low + along, half) if groups % 2 == 0 else lax.rem(group + along, groups)
        for up, along in steps
    ]
    peers = [lax.rem(narrow + offset, narrow_count) for offset in range(1, narrow_count)]

    chunks = values_sem.shape[0]
    chunk = slots // chunks
    value_copies = [
        pltpu.make_async_copy(
            values.at[0, 0, pl.ds(i * chunk, chunk)], blocks.at[pl.ds(i * chunk, chunk)], values_sem.at[i]
        )
        for i in range(chunks)
    ]
    own_copy = pltpu.make_async_copy(features, panel.at[pl.ds(narrow * per_device, per_device)], own_sem)
    for copy in value_copies:
        copy.start()
    own_copy.start()

    barrier = pltpu.get_barrier_semaphore()
    for peer in peers:
        pl.semaphore_signal(barrier, inc=1, device_id={"narrow": peer}, device_id_type=MESH)
    pl.semaphore_signal(barrier, inc=1, device_id={"wide": group * 2 + other}, device_id_type=MESH)
    for target in targets[:-1]:
        pl.semaphore_signal(barrier, inc=1, device_id={"wide": target * 2 + core}, device_id_type=MESH)

    lane = lax.broadcasted_iota(jnp.int32, (1, lanes), 1)
    across = lax.broadcasted_iota(jnp.int32, (lanes, lanes), 1)
    down = lax.broadcasted_iota(jnp.int32, (lanes, lanes), 0)
    order_v[...] = jnp.broadcast_to((tile_rows << row_shift) + lane, order_v.shape)
    slot = lane[:, :slots]
    row = jnp.where(slot < counts[...], rows_in[0], tile_rows)
    order_v[0:1, 0:slots] = (row << row_shift) + (cols_in[0] << col_shift) + slot
    key = order_v[0:1, :]
    key_down = jnp.sum(jnp.where(down == across, key, 0), axis=1, keepdims=True)
    rank = jnp.sum((key < key_down).astype(jnp.int32), axis=1, keepdims=True)
    ordered = jnp.sum(jnp.where(rank == across, key_down, 0), axis=0, keepdims=True)
    row_down = key_down >> row_shift
    upto = jnp.sum((row_down <= across).astype(jnp.int32), axis=0, keepdims=True)
    held = jnp.sum((row_down == across).astype(jnp.int32), axis=0, keepdims=True)
    order_v[0:1, :] = ordered & ((1 << col_shift) - 1)
    order_v[1:2, :] = (ordered >> col_shift) & ((1 << (row_shift - col_shift)) - 1)
    order_v[2:3, :] = ordered >> row_shift
    order_v[3:4, :] = jnp.maximum(upto - 1, 0)
    order_v[4:5, :] = held
    order_copy = pltpu.make_async_copy(order_v, order_s, order_sem)
    order_copy.start()

    pl.semaphore_wait(barrier, (narrow_count - 1) + 1 + (groups - 1))

    feature_copies = []
    for i, peer in enumerate(peers):
        copy = pltpu.make_async_remote_copy(
            src_ref=features,
            dst_ref=panel.at[pl.ds(narrow * per_device, per_device)],
            send_sem=feat_send.at[i],
            recv_sem=feat_recv.at[i],
            device_id={"narrow": peer},
            device_id_type=MESH,
        )
        copy.start()
        feature_copies.append(copy)

    for copy in value_copies:
        copy.wait()
    own_copy.wait()
    order_copy.wait()
    for copy in feature_copies:
        copy.wait_recv()

    unroll = max(u for u in range(1, 9) if slots % u == 0)

    def sweep(step, total):
        for j in range(unroll):
            p = step * unroll + j
            before = jnp.maximum(p - 1, 0)
            keep = jnp.where(order_s[2, p] == order_s[2, before], 1.0, 0.0).astype(jnp.float32)
            product = jnp.dot(blocks[order_s[0, p]], panel[order_s[1, p]], preferred_element_type=jnp.float32)
            total = total * keep + product
            running[p] = total
        return total

    lax.fori_loop(0, slots // unroll, sweep, jnp.zeros((block, width), jnp.float32))

    def row_sum(r):
        present = jnp.where(order_s[4, r] > 0, 1.0, 0.0).astype(jnp.float32)
        return running[order_s[3, r]] * present

    pair_copies = []
    for i, target in enumerate(targets):
        for j in range(per_device):
            pair_out[i, j * block:(j + 1) * block, :] = row_sum((target * 2 + other) * per_device + j)
        copy = pltpu.make_async_remote_copy(
            src_ref=pair_out.at[i],
            dst_ref=pair_in.at[i],
            send_sem=pair_send.at[i],
            recv_sem=pair_recv.at[i],
            device_id={"wide": group * 2 + other},
            device_id_type=MESH,
        )
        copy.start()
        pair_copies.append(copy)

    line_copies = []
    total = None
    for i, target in enumerate(targets):
        own = jnp.concatenate(
            [row_sum((target * 2 + core) * per_device + j) for j in range(per_device)], axis=0
        )
        pair_copies[i].wait_recv()
        both = own + pair_in[i]
        if i == groups - 1:
            total = both
        else:
            line_out[i] = both.astype(jnp.bfloat16)
            copy = pltpu.make_async_remote_copy(
                src_ref=line_out.at[i],
                dst_ref=line_in.at[i],
                send_sem=line_send.at[i],
                recv_sem=line_recv.at[i],
                device_id={"wide": target * 2 + core},
                device_id_type=MESH,
            )
            copy.start()
            line_copies.append(copy)

    for i, copy in enumerate(line_copies):
        copy.wait_recv()
        total = total + line_in[i].astype(jnp.float32)
    mixed = jnp.dot(total.astype(jnp.bfloat16), weight[...], preferred_element_type=jnp.float32) + bias[...]
    out[...] = jnp.maximum(mixed, 0.0).astype(out.dtype)

    for copy in feature_copies + pair_copies + line_copies:
        copy.wait_send()


def dense_kernel(
    wide_count, narrow_count,
    features, values, rows_in, cols_in, counts, weight, bias,
    out,
    panel, blocks, running, dense, sums, order_v, order_s, pair_out, pair_in, line_out, line_in,
    values_sem, own_sem, order_sem, feat_send, feat_recv, pair_send, pair_recv, line_send, line_recv,
):
    nodes, width = features.shape
    slots, block = blocks.shape[0], blocks.shape[1]
    per_device = nodes // block
    tile_rows = wide_count * per_device
    panel_blocks = narrow_count * per_device
    spots = tile_rows * panel_blocks
    groups = wide_count // 2
    half, steps = group_steps(groups)
    lanes = order_v.shape[1]
    shift = bits_for(lanes)

    wide = lax.axis_index("wide")
    narrow = lax.axis_index("narrow")
    group = lax.div(wide, 2)
    core = lax.rem(wide, 2)
    other = 1 - core
    high, low = lax.div(group, half), lax.rem(group, half)
    targets = [
        lax.rem(high + up, 2) * half + lax.rem(low + along, half) if groups % 2 == 0 else lax.rem(group + along, groups)
        for up, along in steps
    ]
    peers = [lax.rem(narrow + offset, narrow_count) for offset in range(1, narrow_count)]

    chunks = values_sem.shape[0]
    chunk = slots // chunks
    value_copies = [
        pltpu.make_async_copy(
            values.at[0, 0, pl.ds(i * chunk, chunk)], blocks.at[pl.ds(i * chunk, chunk)], values_sem.at[i]
        )
        for i in range(chunks)
    ]
    own_copy = pltpu.make_async_copy(features, panel.at[narrow], own_sem)
    for copy in value_copies:
        copy.start()
    own_copy.start()

    barrier = pltpu.get_barrier_semaphore()
    for peer in peers:
        pl.semaphore_signal(barrier, inc=1, device_id={"narrow": peer}, device_id_type=MESH)
    pl.semaphore_signal(barrier, inc=1, device_id={"wide": group * 2 + other}, device_id_type=MESH)
    for target in targets[:-1]:
        pl.semaphore_signal(barrier, inc=1, device_id={"wide": target * 2 + core}, device_id_type=MESH)

    lane = lax.broadcasted_iota(jnp.int32, (1, lanes), 1)
    across = lax.broadcasted_iota(jnp.int32, (lanes, lanes), 1)
    down = lax.broadcasted_iota(jnp.int32, (lanes, lanes), 0)
    order_v[...] = jnp.broadcast_to((spots << shift) + lane, order_v.shape)
    slot = lane[:, :slots]
    spot = jnp.where(slot < counts[...], rows_in[0] * panel_blocks + cols_in[0], spots)
    order_v[0:1, 0:slots] = (spot << shift) + slot
    key = order_v[0:1, :]
    key_down = jnp.sum(jnp.where(down == across, key, 0), axis=1, keepdims=True)
    rank = jnp.sum((key < key_down).astype(jnp.int32), axis=1, keepdims=True)
    ordered = jnp.sum(jnp.where(rank == across, key_down, 0), axis=0, keepdims=True)
    spot_down = key_down >> shift
    upto = jnp.sum((spot_down <= across).astype(jnp.int32), axis=0, keepdims=True)
    held = jnp.sum((spot_down == across).astype(jnp.int32), axis=0, keepdims=True)
    order_v[0:1, :] = ordered & ((1 << shift) - 1)
    order_v[1:2, :] = ordered >> shift
    order_v[2:3, :] = jnp.where(held > 0, upto, 0)
    order_copy = pltpu.make_async_copy(order_v, order_s, order_sem)
    order_copy.start()

    pl.semaphore_wait(barrier, (narrow_count - 1) + 1 + (groups - 1))

    feature_copies = []
    for i, peer in enumerate(peers):
        copy = pltpu.make_async_remote_copy(
            src_ref=features,
            dst_ref=panel.at[narrow],
            send_sem=feat_send.at[i],
            recv_sem=feat_recv.at[i],
            device_id={"narrow": peer},
            device_id_type=MESH,
        )
        copy.start()
        feature_copies.append(copy)

    running[0] = jnp.zeros((block, block), running.dtype)
    order_copy.wait()
    for copy in value_copies:
        copy.wait()
    unroll = max(u for u in range(1, 9) if slots % u == 0)

    def sweep(step, total):
        for j in range(unroll):
            p = step * unroll + j
            keep = jnp.where(order_s[1, p] == order_s[1, jnp.maximum(p - 1, 0)], 1.0, 0.0)
            total = total * keep.astype(jnp.float32) + blocks[order_s[0, p]].astype(jnp.float32)
            running[p + 1] = total.astype(running.dtype)
        return total

    lax.fori_loop(0, slots // unroll, sweep, jnp.zeros((block, block), jnp.float32))

    def place(r, carry):
        for c in range(panel_blocks):
            dense[c // per_device, pl.ds(pl.multiple_of(r * block, block), block),
                  (c % per_device) * block:(c % per_device + 1) * block] = running[order_s[2, r * panel_blocks + c]]
        return carry

    lax.fori_loop(0, tile_rows, place, 0)

    own_copy.wait()

    def multiply(d, carry):
        here = pl.ds(pl.multiple_of(d * nodes, nodes), nodes)
        sums[here] = jnp.dot(dense[narrow, here], panel[narrow], preferred_element_type=jnp.float32)
        return carry

    lax.fori_loop(0, wide_count, multiply, 0, unroll=True)
    for copy in feature_copies:
        copy.wait_recv()

    def chunk_sum(d):
        here = pl.ds(pl.multiple_of(d * nodes, nodes), nodes)
        total = sums[here]
        for source in peers:
            total = total + jnp.dot(dense[source, here], panel[source], preferred_element_type=jnp.float32)
        return total

    pair_copies, line_copies = [], []

    def send_pair(i):
        pair_out[i] = chunk_sum(targets[i] * 2 + other)
        copy = pltpu.make_async_remote_copy(
            src_ref=pair_out.at[i],
            dst_ref=pair_in.at[i],
            send_sem=pair_send.at[i],
            recv_sem=pair_recv.at[i],
            device_id={"wide": group * 2 + other},
            device_id_type=MESH,
        )
        copy.start()
        pair_copies.append(copy)

    def send_line(i):
        own = chunk_sum(targets[i] * 2 + core)
        pair_copies[i].wait_recv()
        line_out[i] = (own + pair_in[i]).astype(jnp.bfloat16)
        copy = pltpu.make_async_remote_copy(
            src_ref=line_out.at[i],
            dst_ref=line_in.at[i],
            send_sem=line_send.at[i],
            recv_sem=line_recv.at[i],
            device_id={"wide": targets[i] * 2 + core},
            device_id_type=MESH,
        )
        copy.start()
        line_copies.append(copy)

    for i in range(min(2, groups)):
        send_pair(i)
    for i in range(groups - 1):
        send_line(i)
        if i + 2 < groups:
            send_pair(i + 2)
    total = chunk_sum(targets[-1] * 2 + core)
    pair_copies[-1].wait_recv()
    total = total + pair_in[groups - 1]

    for i, copy in enumerate(line_copies):
        copy.wait_recv()
        total = total + line_in[i].astype(jnp.float32)
    mixed = jnp.dot(total.astype(jnp.bfloat16), weight[...], preferred_element_type=jnp.float32) + bias[...]
    out[...] = jnp.maximum(mixed, 0.0).astype(out.dtype)

    for copy in feature_copies + pair_copies + line_copies:
        copy.wait_send()


DENSE_BYTES = 8 * 1024 * 1024


def shards(features, block_values, block_rows, block_cols, counts, weight, bias):
    wide_count = lax.axis_size("wide")
    narrow_count = lax.axis_size("narrow")
    nodes, width = features.shape
    slots, block = block_values.shape[2], block_values.shape[3]
    per_device = nodes // block
    groups = wide_count // 2
    hidden = weight.shape[1]
    tile_rows = wide_count * per_device
    panel_blocks = narrow_count * per_device
    dense_fits = tile_rows * panel_blocks * block * block * 2 <= DENSE_BYTES
    keys = tile_rows * panel_blocks if dense_fits else tile_rows
    lanes = -(-max(slots, keys) // 128) * 128
    chunks = max(c for c in (1, 2, 4) if slots % c == 0)
    others = max(narrow_count - 1, 1)
    in_vmem = pl.BlockSpec(memory_space=pltpu.VMEM)
    in_hbm = pl.BlockSpec(memory_space=pltpu.HBM)
    dma = pltpu.SemaphoreType.DMA
    return pl.pallas_call(
        functools.partial(dense_kernel if dense_fits else slot_kernel, wide_count, narrow_count),
        out_shape=jax.ShapeDtypeStruct((nodes, hidden), jnp.bfloat16),
        in_specs=[in_hbm, in_hbm] + [in_vmem] * 5,
        out_specs=in_vmem,
        scratch_shapes=[
            *(
                [
                    pltpu.VMEM((narrow_count, nodes, width), jnp.bfloat16),
                    pltpu.VMEM((slots, block, block), jnp.bfloat16),
                    pltpu.VMEM((slots + 1, block, block), jnp.bfloat16),
                    pltpu.VMEM((narrow_count, wide_count * nodes, nodes), jnp.bfloat16),
                    pltpu.VMEM((wide_count * nodes, width), jnp.float32),
                ]
                if dense_fits
                else [
                    pltpu.VMEM((panel_blocks, block, width), jnp.bfloat16),
                    pltpu.VMEM((slots, block, block), jnp.bfloat16),
                    pltpu.VMEM((slots, block, width), jnp.float32),
                ]
            ),
            pltpu.VMEM((8, lanes), jnp.int32),
            pltpu.SMEM((8, lanes), jnp.int32),
            pltpu.VMEM((groups, nodes, width), jnp.float32),
            pltpu.VMEM((groups, nodes, width), jnp.float32),
            pltpu.VMEM((max(groups - 1, 1), nodes, width), jnp.bfloat16),
            pltpu.VMEM((max(groups - 1, 1), nodes, width), jnp.bfloat16),
            dma((chunks,)),
            dma,
            dma,
            dma((others,)),
            dma((others,)),
            dma((groups,)),
            dma((groups,)),
            dma((max(groups - 1, 1),)),
            dma((max(groups - 1, 1),)),
        ],
        compiler_params=pltpu.CompilerParams(
            collective_id=0 if dense_fits else 1, has_side_effects=True, vmem_limit_bytes=56 * 1024 * 1024
        ),
        cost_estimate=pl.CostEstimate(
            flops=2 * slots * block * block * width, bytes_accessed=2 * slots * block * block, transcendentals=0
        ),
    )(
        features if dense_fits else features.reshape(per_device, block, width), block_values, block_rows, block_cols, counts,
        weight, bias.reshape(1, hidden),
    )


def solution(mesh):
    placed = (
        P(("wide", "narrow"), None),
        P("narrow", "wide", None, None, None),
        P("narrow", "wide", None),
        P("narrow", "wide", None),
        P("narrow", "wide"),
        P(),
        P(),
    )
    return jax.shard_map(
        shards, mesh=mesh, in_specs=placed, out_specs=P(("narrow", "wide"), None), check_vma=False
    )
```

```python
import functools

import jax
import jax.numpy as jnp
from jax import lax
from jax.experimental import pallas as pl
from jax.experimental.pallas import tpu as pltpu
from jax.sharding import PartitionSpec as P

MESH = pl.DeviceIdType.MESH


def bits_for(count):
    return max(1, (count - 1).bit_length())


def group_steps(groups):
    if groups % 2 == 0:
        half = groups // 2
        pairs = [(1, low) for low in range(half)] + [(0, low) for low in range(1, half)] + [(0, 0)]
        return half, pairs
    return groups, [(0, low) for low in range(1, groups)] + [(0, 0)]


def slot_kernel(
    wide_count, narrow_count,
    features, values, rows_in, cols_in, counts, weight, bias,
    out,
    panel, blocks, running, order_v, order_s, pair_out, pair_in, line_out, line_in,
    values_sem, own_sem, order_sem, feat_send, feat_recv, pair_send, pair_recv, line_send, line_recv,
):
    per_device, block, width = features.shape
    slots = blocks.shape[0]
    tile_rows = wide_count * per_device
    panel_blocks = narrow_count * per_device
    groups = wide_count // 2
    half, steps = group_steps(groups)
    lanes = order_v.shape[1]
    col_shift = bits_for(lanes)
    row_shift = col_shift + bits_for(panel_blocks)

    wide = lax.axis_index("wide")
    narrow = lax.axis_index("narrow")
    group = lax.div(wide, 2)
    core = lax.rem(wide, 2)
    other = 1 - core
    high, low = lax.div(group, half), lax.rem(group, half)
    targets = [
        lax.rem(high + up, 2) * half + lax.rem(low + along, half) if groups % 2 == 0 else lax.rem(group + along, groups)
        for up, along in steps
    ]
    peers = [lax.rem(narrow + offset, narrow_count) for offset in range(1, narrow_count)]

    chunks = values_sem.shape[0]
    chunk = slots // chunks
    value_copies = [
        pltpu.make_async_copy(
            values.at[0, 0, pl.ds(i * chunk, chunk)], blocks.at[pl.ds(i * chunk, chunk)], values_sem.at[i]
        )
        for i in range(chunks)
    ]
    own_copy = pltpu.make_async_copy(features, panel.at[pl.ds(narrow * per_device, per_device)], own_sem)
    for copy in value_copies:
        copy.start()
    own_copy.start()

    barrier = pltpu.get_barrier_semaphore()
    for peer in peers:
        pl.semaphore_signal(barrier, inc=1, device_id={"narrow": peer}, device_id_type=MESH)
    pl.semaphore_signal(barrier, inc=1, device_id={"wide": group * 2 + other}, device_id_type=MESH)
    for target in targets[:-1]:
        pl.semaphore_signal(barrier, inc=1, device_id={"wide": target * 2 + core}, device_id_type=MESH)

    lane = lax.broadcasted_iota(jnp.int32, (1, lanes), 1)
    across = lax.broadcasted_iota(jnp.int32, (lanes, lanes), 1)
    down = lax.broadcasted_iota(jnp.int32, (lanes, lanes), 0)
    order_v[...] = jnp.broadcast_to((tile_rows << row_shift) + lane, order_v.shape)
    slot = lane[:, :slots]
    row = jnp.where(slot < counts[...], rows_in[0], tile_rows)
    order_v[0:1, 0:slots] = (row << row_shift) + (cols_in[0] << col_shift) + slot
    key = order_v[0:1, :]
    key_down = jnp.sum(jnp.where(down == across, key, 0), axis=1, keepdims=True)
    rank = jnp.sum((key < key_down).astype(jnp.int32), axis=1, keepdims=True)
    ordered = jnp.sum(jnp.where(rank == across, key_down, 0), axis=0, keepdims=True)
    row_down = key_down >> row_shift
    upto = jnp.sum((row_down <= across).astype(jnp.int32), axis=0, keepdims=True)
    held = jnp.sum((row_down == across).astype(jnp.int32), axis=0, keepdims=True)
    order_v[0:1, :] = ordered & ((1 << col_shift) - 1)
    order_v[1:2, :] = (ordered >> col_shift) & ((1 << (row_shift - col_shift)) - 1)
    order_v[2:3, :] = ordered >> row_shift
    order_v[3:4, :] = jnp.maximum(upto - 1, 0)
    order_v[4:5, :] = held
    order_copy = pltpu.make_async_copy(order_v, order_s, order_sem)
    order_copy.start()

    pl.semaphore_wait(barrier, (narrow_count - 1) + 1 + (groups - 1))

    feature_copies = []
    for i, peer in enumerate(peers):
        copy = pltpu.make_async_remote_copy(
            src_ref=features,
            dst_ref=panel.at[pl.ds(narrow * per_device, per_device)],
            send_sem=feat_send.at[i],
            recv_sem=feat_recv.at[i],
            device_id={"narrow": peer},
            device_id_type=MESH,
        )
        copy.start()
        feature_copies.append(copy)

    for copy in value_copies:
        copy.wait()
    own_copy.wait()
    order_copy.wait()
    for copy in feature_copies:
        copy.wait_recv()

    unroll = max(u for u in range(1, 9) if slots % u == 0)

    def sweep(step, total):
        for j in range(unroll):
            p = step * unroll + j
            before = jnp.maximum(p - 1, 0)
            keep = jnp.where(order_s[2, p] == order_s[2, before], 1.0, 0.0).astype(jnp.float32)
            product = jnp.dot(blocks[order_s[0, p]], panel[order_s[1, p]], preferred_element_type=jnp.float32)
            total = total * keep + product
            running[p] = total
        return total

    lax.fori_loop(0, slots // unroll, sweep, jnp.zeros((block, width), jnp.float32))

    def row_sum(r):
        present = jnp.where(order_s[4, r] > 0, 1.0, 0.0).astype(jnp.float32)
        return running[order_s[3, r]] * present

    pair_copies = []
    for i, target in enumerate(targets):
        for j in range(per_device):
            pair_out[i, j * block:(j + 1) * block, :] = row_sum((target * 2 + other) * per_device + j)
        copy = pltpu.make_async_remote_copy(
            src_ref=pair_out.at[i],
            dst_ref=pair_in.at[i],
            send_sem=pair_send.at[i],
            recv_sem=pair_recv.at[i],
            device_id={"wide": group * 2 + other},
            device_id_type=MESH,
        )
        copy.start()
        pair_copies.append(copy)

    line_copies = []
    total = None
    for i, target in enumerate(targets):
        own = jnp.concatenate(
            [row_sum((target * 2 + core) * per_device + j) for j in range(per_device)], axis=0
        )
        pair_copies[i].wait_recv()
        both = own + pair_in[i]
        if i == groups - 1:
            total = both
        else:
            line_out[i] = both.astype(jnp.bfloat16)
            copy = pltpu.make_async_remote_copy(
                src_ref=line_out.at[i],
                dst_ref=line_in.at[i],
                send_sem=line_send.at[i],
                recv_sem=line_recv.at[i],
                device_id={"wide": target * 2 + core},
                device_id_type=MESH,
            )
            copy.start()
            line_copies.append(copy)

    for i, copy in enumerate(line_copies):
        copy.wait_recv()
        total = total + line_in[i].astype(jnp.float32)
    mixed = jnp.dot(total.astype(jnp.bfloat16), weight[...], preferred_element_type=jnp.float32) + bias[...]
    out[...] = jnp.maximum(mixed, 0.0).astype(out.dtype)

    for copy in feature_copies + pair_copies + line_copies:
        copy.wait_send()


def dense_kernel(
    wide_count, narrow_count,
    features, values, rows_in, cols_in, counts, weight, bias,
    out,
    panel, blocks, running, dense, sums, order_v, order_s, pair_out, pair_in, line_out, line_in,
    values_sem, own_sem, order_sem, feat_send, feat_recv, pair_send, pair_recv, line_send, line_recv,
):
    nodes, width = features.shape
    slots, block = blocks.shape[0], blocks.shape[1]
    per_device = nodes // block
    tile_rows = wide_count * per_device
    panel_blocks = narrow_count * per_device
    spots = tile_rows * panel_blocks
    groups = wide_count // 2
    half, steps = group_steps(groups)
    lanes = order_v.shape[1]
    shift = bits_for(lanes)

    wide = lax.axis_index("wide")
    narrow = lax.axis_index("narrow")
    group = lax.div(wide, 2)
    core = lax.rem(wide, 2)
    other = 1 - core
    high, low = lax.div(group, half), lax.rem(group, half)
    targets = [
        lax.rem(high + up, 2) * half + lax.rem(low + along, half) if groups % 2 == 0 else lax.rem(group + along, groups)
        for up, along in steps
    ]
    peers = [lax.rem(narrow + offset, narrow_count) for offset in range(1, narrow_count)]

    chunks = values_sem.shape[0]
    chunk = slots // chunks
    value_copies = [
        pltpu.make_async_copy(
            values.at[0, 0, pl.ds(i * chunk, chunk)], blocks.at[pl.ds(i * chunk, chunk)], values_sem.at[i]
        )
        for i in range(chunks)
    ]
    own_copy = pltpu.make_async_copy(features, panel.at[narrow], own_sem)
    for copy in value_copies:
        copy.start()
    own_copy.start()

    barrier = pltpu.get_barrier_semaphore()
    for peer in peers:
        pl.semaphore_signal(barrier, inc=1, device_id={"narrow": peer}, device_id_type=MESH)
    pl.semaphore_signal(barrier, inc=1, device_id={"wide": group * 2 + other}, device_id_type=MESH)
    for target in targets[:-1]:
        pl.semaphore_signal(barrier, inc=1, device_id={"wide": target * 2 + core}, device_id_type=MESH)

    lane = lax.broadcasted_iota(jnp.int32, (1, lanes), 1)
    across = lax.broadcasted_iota(jnp.int32, (lanes, lanes), 1)
    down = lax.broadcasted_iota(jnp.int32, (lanes, lanes), 0)
    order_v[...] = jnp.broadcast_to((spots << shift) + lane, order_v.shape)
    slot = lane[:, :slots]
    spot = jnp.where(slot < counts[...], rows_in[0] * panel_blocks + cols_in[0], spots)
    order_v[0:1, 0:slots] = (spot << shift) + slot
    key = order_v[0:1, :]
    key_down = jnp.sum(jnp.where(down == across, key, 0), axis=1, keepdims=True)
    rank = jnp.sum((key < key_down).astype(jnp.int32), axis=1, keepdims=True)
    ordered = jnp.sum(jnp.where(rank == across, key_down, 0), axis=0, keepdims=True)
    spot_down = key_down >> shift
    upto = jnp.sum((spot_down <= across).astype(jnp.int32), axis=0, keepdims=True)
    held = jnp.sum((spot_down == across).astype(jnp.int32), axis=0, keepdims=True)
    order_v[0:1, :] = ordered & ((1 << shift) - 1)
    order_v[1:2, :] = ordered >> shift
    order_v[2:3, :] = jnp.where(held > 0, upto, 0)
    order_copy = pltpu.make_async_copy(order_v, order_s, order_sem)
    order_copy.start()

    pl.semaphore_wait(barrier, (narrow_count - 1) + 1 + (groups - 1))

    feature_copies = []
    for i, peer in enumerate(peers):
        copy = pltpu.make_async_remote_copy(
            src_ref=features,
            dst_ref=panel.at[narrow],
            send_sem=feat_send.at[i],
            recv_sem=feat_recv.at[i],
            device_id={"narrow": peer},
            device_id_type=MESH,
        )
        copy.start()
        feature_copies.append(copy)

    running[0] = jnp.zeros((block, block), running.dtype)
    order_copy.wait()
    for copy in value_copies:
        copy.wait()
    unroll = max(u for u in range(1, 9) if slots % u == 0)

    def sweep(step, total):
        for j in range(unroll):
            p = step * unroll + j
            keep = jnp.where(order_s[1, p] == order_s[1, jnp.maximum(p - 1, 0)], 1.0, 0.0)
            total = total * keep.astype(jnp.float32) + blocks[order_s[0, p]].astype(jnp.float32)
            running[p + 1] = total.astype(running.dtype)
        return total

    lax.fori_loop(0, slots // unroll, sweep, jnp.zeros((block, block), jnp.float32))

    def place(r, carry):
        for c in range(panel_blocks):
            dense[c // per_device, pl.ds(pl.multiple_of(r * block, block), block),
                  (c % per_device) * block:(c % per_device + 1) * block] = running[order_s[2, r * panel_blocks + c]]
        return carry

    lax.fori_loop(0, tile_rows, place, 0)

    own_copy.wait()

    def multiply(d, carry):
        here = pl.ds(pl.multiple_of(d * nodes, nodes), nodes)
        sums[here] = jnp.dot(dense[narrow, here], panel[narrow], preferred_element_type=jnp.float32)
        return carry

    lax.fori_loop(0, wide_count, multiply, 0, unroll=True)
    for copy in feature_copies:
        copy.wait_recv()

    def chunk_sum(d):
        here = pl.ds(pl.multiple_of(d * nodes, nodes), nodes)
        total = sums[here]
        for source in peers:
            total = total + jnp.dot(dense[source, here], panel[source], preferred_element_type=jnp.float32)
        return total

    pair_copies, line_copies = {}, []

    def send_pair(i):
        pair_out[i] = chunk_sum(targets[i] * 2 + other)
        copy = pltpu.make_async_remote_copy(
            src_ref=pair_out.at[i],
            dst_ref=pair_in.at[i],
            send_sem=pair_send.at[i],
            recv_sem=pair_recv.at[i],
            device_id={"wide": group * 2 + other},
            device_id_type=MESH,
        )
        copy.start()
        pair_copies[i] = copy

    def chip_sum(i):
        own = chunk_sum(targets[i] * 2 + core)
        pair_copies[i].wait_recv()
        return own + pair_in[i]

    def send_line(i, value, target):
        line_out[i] = value.astype(jnp.bfloat16)
        copy = pltpu.make_async_remote_copy(
            src_ref=line_out.at[i],
            dst_ref=line_in.at[i],
            send_sem=line_send.at[i],
            recv_sem=line_recv.at[i],
            device_id={"wide": target * 2 + core},
            device_id_type=MESH,
        )
        copy.start()
        line_copies.append(copy)

    if groups == 4:
        far, near = targets[0], targets[2]
        send_pair(1)
        send_pair(0)
        send_line(0, chip_sum(1), near)
        send_pair(2)
        crossing = chip_sum(0)
        send_line(1, chip_sum(2), near)
        send_pair(3)
        line_copies[0].wait_recv()
        send_line(2, crossing + line_in[0].astype(jnp.float32), far)
        total = chip_sum(3)
        arriving = (1, 2)
    else:
        for i in range(min(2, groups)):
            send_pair(i)
        for i in range(groups - 1):
            send_line(i, chip_sum(i), targets[i])
            if i + 2 < groups:
                send_pair(i + 2)
        total = chip_sum(groups - 1)
        arriving = range(groups - 1)

    for i in arriving:
        line_copies[i].wait_recv()
        total = total + line_in[i].astype(jnp.float32)
    mixed = jnp.dot(total.astype(jnp.bfloat16), weight[...], preferred_element_type=jnp.float32) + bias[...]
    out[...] = jnp.maximum(mixed, 0.0).astype(out.dtype)

    for copy in feature_copies + list(pair_copies.values()) + line_copies:
        copy.wait_send()


DENSE_BYTES = 8 * 1024 * 1024


def shards(features, block_values, block_rows, block_cols, counts, weight, bias):
    wide_count = lax.axis_size("wide")
    narrow_count = lax.axis_size("narrow")
    nodes, width = features.shape
    slots, block = block_values.shape[2], block_values.shape[3]
    per_device = nodes // block
    groups = wide_count // 2
    hidden = weight.shape[1]
    tile_rows = wide_count * per_device
    panel_blocks = narrow_count * per_device
    dense_fits = tile_rows * panel_blocks * block * block * 2 <= DENSE_BYTES
    keys = tile_rows * panel_blocks if dense_fits else tile_rows
    lanes = -(-max(slots, keys) // 128) * 128
    chunks = max(c for c in (1, 2, 4) if slots % c == 0)
    others = max(narrow_count - 1, 1)
    in_vmem = pl.BlockSpec(memory_space=pltpu.VMEM)
    in_hbm = pl.BlockSpec(memory_space=pltpu.HBM)
    dma = pltpu.SemaphoreType.DMA
    return pl.pallas_call(
        functools.partial(dense_kernel if dense_fits else slot_kernel, wide_count, narrow_count),
        out_shape=jax.ShapeDtypeStruct((nodes, hidden), jnp.bfloat16),
        in_specs=[in_hbm, in_hbm] + [in_vmem] * 5,
        out_specs=in_vmem,
        scratch_shapes=[
            *(
                [
                    pltpu.VMEM((narrow_count, nodes, width), jnp.bfloat16),
                    pltpu.VMEM((slots, block, block), jnp.bfloat16),
                    pltpu.VMEM((slots + 1, block, block), jnp.bfloat16),
                    pltpu.VMEM((narrow_count, wide_count * nodes, nodes), jnp.bfloat16),
                    pltpu.VMEM((wide_count * nodes, width), jnp.float32),
                ]
                if dense_fits
                else [
                    pltpu.VMEM((panel_blocks, block, width), jnp.bfloat16),
                    pltpu.VMEM((slots, block, block), jnp.bfloat16),
                    pltpu.VMEM((slots, block, width), jnp.float32),
                ]
            ),
            pltpu.VMEM((8, lanes), jnp.int32),
            pltpu.SMEM((8, lanes), jnp.int32),
            pltpu.VMEM((groups, nodes, width), jnp.float32),
            pltpu.VMEM((groups, nodes, width), jnp.float32),
            pltpu.VMEM((max(groups - 1, 1), nodes, width), jnp.bfloat16),
            pltpu.VMEM((max(groups - 1, 1), nodes, width), jnp.bfloat16),
            dma((chunks,)),
            dma,
            dma,
            dma((others,)),
            dma((others,)),
            dma((groups,)),
            dma((groups,)),
            dma((max(groups - 1, 1),)),
            dma((max(groups - 1, 1),)),
        ],
        compiler_params=pltpu.CompilerParams(
            collective_id=0 if dense_fits else 1, has_side_effects=True, vmem_limit_bytes=56 * 1024 * 1024
        ),
        cost_estimate=pl.CostEstimate(
            flops=2 * slots * block * block * width, bytes_accessed=2 * slots * block * block, transcendentals=0
        ),
    )(
        features if dense_fits else features.reshape(per_device, block, width), block_values, block_rows, block_cols, counts,
        weight, bias.reshape(1, hidden),
    )


def solution(mesh):
    placed = (
        P(("wide", "narrow"), None),
        P("narrow", "wide", None, None, None),
        P("narrow", "wide", None),
        P("narrow", "wide", None),
        P("narrow", "wide"),
        P(),
        P(),
    )
    return jax.shard_map(
        shards, mesh=mesh, in_specs=placed, out_specs=P(("narrow", "wide"), None), check_vma=False
    )
```

```python
import functools

import jax
import jax.numpy as jnp
from jax import lax
from jax.experimental import pallas as pl
from jax.experimental.pallas import tpu as pltpu
from jax.sharding import PartitionSpec as P

MESH = pl.DeviceIdType.MESH


def bits_for(count):
    return max(1, (count - 1).bit_length())


def group_steps(groups):
    if groups % 2 == 0:
        half = groups // 2
        pairs = [(1, low) for low in range(half)] + [(0, low) for low in range(1, half)] + [(0, 0)]
        return half, pairs
    return groups, [(0, low) for low in range(1, groups)] + [(0, 0)]


def slot_kernel(
    wide_count, narrow_count,
    features, values, rows_in, cols_in, counts, weight, bias,
    out,
    panel, blocks, running, order_v, order_s, pair_out, pair_in, line_out, line_in,
    values_sem, own_sem, order_sem, feat_send, feat_recv, pair_send, pair_recv, line_send, line_recv,
):
    per_device, block, width = features.shape
    slots = blocks.shape[0]
    tile_rows = wide_count * per_device
    panel_blocks = narrow_count * per_device
    groups = wide_count // 2
    half, steps = group_steps(groups)
    lanes = order_v.shape[1]
    col_shift = bits_for(lanes)
    row_shift = col_shift + bits_for(panel_blocks)

    wide = lax.axis_index("wide")
    narrow = lax.axis_index("narrow")
    group = lax.div(wide, 2)
    core = lax.rem(wide, 2)
    other = 1 - core
    high, low = lax.div(group, half), lax.rem(group, half)
    targets = [
        lax.rem(high + up, 2) * half + lax.rem(low + along, half) if groups % 2 == 0 else lax.rem(group + along, groups)
        for up, along in steps
    ]
    peers = [lax.rem(narrow + offset, narrow_count) for offset in range(1, narrow_count)]

    chunks = values_sem.shape[0]
    chunk = slots // chunks
    value_copies = [
        pltpu.make_async_copy(
            values.at[0, 0, pl.ds(i * chunk, chunk)], blocks.at[pl.ds(i * chunk, chunk)], values_sem.at[i]
        )
        for i in range(chunks)
    ]
    own_copy = pltpu.make_async_copy(features, panel.at[pl.ds(narrow * per_device, per_device)], own_sem)
    for copy in value_copies:
        copy.start()
    own_copy.start()

    barrier = pltpu.get_barrier_semaphore()
    for peer in peers:
        pl.semaphore_signal(barrier, inc=1, device_id={"narrow": peer}, device_id_type=MESH)
    pl.semaphore_signal(barrier, inc=1, device_id={"wide": group * 2 + other}, device_id_type=MESH)
    for target in targets[:-1]:
        pl.semaphore_signal(barrier, inc=1, device_id={"wide": target * 2 + core}, device_id_type=MESH)

    lane = lax.broadcasted_iota(jnp.int32, (1, lanes), 1)
    across = lax.broadcasted_iota(jnp.int32, (lanes, lanes), 1)
    down = lax.broadcasted_iota(jnp.int32, (lanes, lanes), 0)
    order_v[...] = jnp.broadcast_to((tile_rows << row_shift) + lane, order_v.shape)
    slot = lane[:, :slots]
    row = jnp.where(slot < counts[...], rows_in[0], tile_rows)
    order_v[0:1, 0:slots] = (row << row_shift) + (cols_in[0] << col_shift) + slot
    key = order_v[0:1, :]
    key_down = jnp.sum(jnp.where(down == across, key, 0), axis=1, keepdims=True)
    rank = jnp.sum((key < key_down).astype(jnp.int32), axis=1, keepdims=True)
    ordered = jnp.sum(jnp.where(rank == across, key_down, 0), axis=0, keepdims=True)
    row_down = key_down >> row_shift
    upto = jnp.sum((row_down <= across).astype(jnp.int32), axis=0, keepdims=True)
    held = jnp.sum((row_down == across).astype(jnp.int32), axis=0, keepdims=True)
    order_v[0:1, :] = ordered & ((1 << col_shift) - 1)
    order_v[1:2, :] = (ordered >> col_shift) & ((1 << (row_shift - col_shift)) - 1)
    order_v[2:3, :] = ordered >> row_shift
    order_v[3:4, :] = jnp.maximum(upto - 1, 0)
    order_v[4:5, :] = held
    order_copy = pltpu.make_async_copy(order_v, order_s, order_sem)
    order_copy.start()

    pl.semaphore_wait(barrier, (narrow_count - 1) + 1 + (groups - 1))

    feature_copies = []
    for i, peer in enumerate(peers):
        copy = pltpu.make_async_remote_copy(
            src_ref=features,
            dst_ref=panel.at[pl.ds(narrow * per_device, per_device)],
            send_sem=feat_send.at[i],
            recv_sem=feat_recv.at[i],
            device_id={"narrow": peer},
            device_id_type=MESH,
        )
        copy.start()
        feature_copies.append(copy)

    for copy in value_copies:
        copy.wait()
    own_copy.wait()
    order_copy.wait()
    for copy in feature_copies:
        copy.wait_recv()

    unroll = max(u for u in range(1, 9) if slots % u == 0)

    def sweep(step, total):
        for j in range(unroll):
            p = step * unroll + j
            before = jnp.maximum(p - 1, 0)
            keep = jnp.where(order_s[2, p] == order_s[2, before], 1.0, 0.0).astype(jnp.float32)
            product = jnp.dot(blocks[order_s[0, p]], panel[order_s[1, p]], preferred_element_type=jnp.float32)
            total = total * keep + product
            running[p] = total
        return total

    lax.fori_loop(0, slots // unroll, sweep, jnp.zeros((block, width), jnp.float32))

    def row_sum(r):
        present = jnp.where(order_s[4, r] > 0, 1.0, 0.0).astype(jnp.float32)
        return running[order_s[3, r]] * present

    pair_copies = []
    for i, target in enumerate(targets):
        for j in range(per_device):
            pair_out[i, j * block:(j + 1) * block, :] = row_sum((target * 2 + other) * per_device + j)
        copy = pltpu.make_async_remote_copy(
            src_ref=pair_out.at[i],
            dst_ref=pair_in.at[i],
            send_sem=pair_send.at[i],
            recv_sem=pair_recv.at[i],
            device_id={"wide": group * 2 + other},
            device_id_type=MESH,
        )
        copy.start()
        pair_copies.append(copy)

    line_copies = []
    total = None
    for i, target in enumerate(targets):
        own = jnp.concatenate(
            [row_sum((target * 2 + core) * per_device + j) for j in range(per_device)], axis=0
        )
        pair_copies[i].wait_recv()
        both = own + pair_in[i]
        if i == groups - 1:
            total = both
        else:
            line_out[i] = both.astype(jnp.bfloat16)
            copy = pltpu.make_async_remote_copy(
                src_ref=line_out.at[i],
                dst_ref=line_in.at[i],
                send_sem=line_send.at[i],
                recv_sem=line_recv.at[i],
                device_id={"wide": target * 2 + core},
                device_id_type=MESH,
            )
            copy.start()
            line_copies.append(copy)

    for i, copy in enumerate(line_copies):
        copy.wait_recv()
        total = total + line_in[i].astype(jnp.float32)
    mixed = jnp.dot(total.astype(jnp.bfloat16), weight[...], preferred_element_type=jnp.float32) + bias[...]
    out[...] = jnp.maximum(mixed, 0.0).astype(out.dtype)

    for copy in feature_copies + pair_copies + line_copies:
        copy.wait_send()


def dense_kernel(
    wide_count, narrow_count,
    features, values, rows_in, cols_in, counts, weight, bias,
    out,
    panel, blocks, running, dense, sums, order_v, order_s, pair_out, pair_in, line_out, line_in,
    values_sem, own_sem, order_sem, feat_send, feat_recv, pair_send, pair_recv, line_send, line_recv,
):
    nodes, width = features.shape
    slots, block = blocks.shape[0], blocks.shape[1]
    per_device = nodes // block
    tile_rows = wide_count * per_device
    panel_blocks = narrow_count * per_device
    spots = tile_rows * panel_blocks
    groups = wide_count // 2
    half, steps = group_steps(groups)
    lanes = order_v.shape[1]
    shift = bits_for(lanes)

    wide = lax.axis_index("wide")
    narrow = lax.axis_index("narrow")
    group = lax.div(wide, 2)
    core = lax.rem(wide, 2)
    other = 1 - core
    high, low = lax.div(group, half), lax.rem(group, half)
    targets = [
        lax.rem(high + up, 2) * half + lax.rem(low + along, half) if groups % 2 == 0 else lax.rem(group + along, groups)
        for up, along in steps
    ]
    peers = [lax.rem(narrow + offset, narrow_count) for offset in range(1, narrow_count)]

    chunks = values_sem.shape[0]
    chunk = slots // chunks
    value_copies = [
        pltpu.make_async_copy(
            values.at[0, 0, pl.ds(i * chunk, chunk)], blocks.at[pl.ds(i * chunk, chunk)], values_sem.at[i]
        )
        for i in range(chunks)
    ]
    own_copy = pltpu.make_async_copy(features, panel.at[narrow], own_sem)
    for copy in value_copies:
        copy.start()
    own_copy.start()

    barrier = pltpu.get_barrier_semaphore()
    for peer in peers:
        pl.semaphore_signal(barrier, inc=1, device_id={"narrow": peer}, device_id_type=MESH)
    pl.semaphore_signal(barrier, inc=1, device_id={"wide": group * 2 + other}, device_id_type=MESH)
    for target in targets[:-1]:
        pl.semaphore_signal(barrier, inc=1, device_id={"wide": target * 2 + core}, device_id_type=MESH)

    lane = lax.broadcasted_iota(jnp.int32, (1, lanes), 1)
    across = lax.broadcasted_iota(jnp.int32, (lanes, lanes), 1)
    down = lax.broadcasted_iota(jnp.int32, (lanes, lanes), 0)
    order_v[...] = jnp.broadcast_to((spots << shift) + lane, order_v.shape)
    slot = lane[:, :slots]
    spot = jnp.where(slot < counts[...], rows_in[0] * panel_blocks + cols_in[0], spots)
    order_v[0:1, 0:slots] = (spot << shift) + slot
    key = order_v[0:1, :]
    key_down = jnp.sum(jnp.where(down == across, key, 0), axis=1, keepdims=True)
    rank = jnp.sum((key < key_down).astype(jnp.int32), axis=1, keepdims=True)
    ordered = jnp.sum(jnp.where(rank == across, key_down, 0), axis=0, keepdims=True)
    spot_down = key_down >> shift
    upto = jnp.sum((spot_down <= across).astype(jnp.int32), axis=0, keepdims=True)
    held = jnp.sum((spot_down == across).astype(jnp.int32), axis=0, keepdims=True)
    order_v[0:1, :] = ordered & ((1 << shift) - 1)
    order_v[1:2, :] = ordered >> shift
    order_v[2:3, :] = jnp.where(held > 0, upto, 0)
    order_copy = pltpu.make_async_copy(order_v, order_s, order_sem)
    order_copy.start()

    pl.semaphore_wait(barrier, (narrow_count - 1) + 1 + (groups - 1))

    feature_copies = []
    for i, peer in enumerate(peers):
        copy = pltpu.make_async_remote_copy(
            src_ref=features,
            dst_ref=panel.at[narrow],
            send_sem=feat_send.at[i],
            recv_sem=feat_recv.at[i],
            device_id={"narrow": peer},
            device_id_type=MESH,
        )
        copy.start()
        feature_copies.append(copy)

    running[0] = jnp.zeros((block, block), running.dtype)
    order_copy.wait()
    for copy in value_copies:
        copy.wait()
    unroll = max(u for u in range(1, 9) if slots % u == 0)

    def sweep(step, total):
        for j in range(unroll):
            p = step * unroll + j
            keep = jnp.where(order_s[1, p] == order_s[1, jnp.maximum(p - 1, 0)], 1.0, 0.0)
            total = total * keep.astype(jnp.float32) + blocks[order_s[0, p]].astype(jnp.float32)
            running[p + 1] = total.astype(running.dtype)
        return total

    lax.fori_loop(0, slots // unroll, sweep, jnp.zeros((block, block), jnp.float32))

    def place(r, carry):
        for c in range(panel_blocks):
            dense[c // per_device, pl.ds(pl.multiple_of(r * block, block), block),
                  (c % per_device) * block:(c % per_device + 1) * block] = running[order_s[2, r * panel_blocks + c]]
        return carry

    lax.fori_loop(0, tile_rows, place, 0)

    own_copy.wait()

    def multiply(d, carry):
        here = pl.ds(pl.multiple_of(d * nodes, nodes), nodes)
        sums[here] = jnp.dot(dense[narrow, here], panel[narrow], preferred_element_type=jnp.float32)
        return carry

    lax.fori_loop(0, wide_count, multiply, 0, unroll=True)
    for copy in feature_copies:
        copy.wait_recv()

    def chunk_sum(d):
        here = pl.ds(pl.multiple_of(d * nodes, nodes), nodes)
        total = sums[here]
        for source in peers:
            total = total + jnp.dot(dense[source, here], panel[source], preferred_element_type=jnp.float32)
        return total

    pair_copies, line_copies = [], []

    def send_pair(i):
        pair_out[i] = chunk_sum(targets[i] * 2 + other).astype(pair_out.dtype)
        copy = pltpu.make_async_remote_copy(
            src_ref=pair_out.at[i],
            dst_ref=pair_in.at[i],
            send_sem=pair_send.at[i],
            recv_sem=pair_recv.at[i],
            device_id={"wide": group * 2 + other},
            device_id_type=MESH,
        )
        copy.start()
        pair_copies.append(copy)

    def send_line(i):
        own = chunk_sum(targets[i] * 2 + core)
        pair_copies[i].wait_recv()
        line_out[i] = (own + pair_in[i].astype(jnp.float32)).astype(jnp.bfloat16)
        copy = pltpu.make_async_remote_copy(
            src_ref=line_out.at[i],
            dst_ref=line_in.at[i],
            send_sem=line_send.at[i],
            recv_sem=line_recv.at[i],
            device_id={"wide": targets[i] * 2 + core},
            device_id_type=MESH,
        )
        copy.start()
        line_copies.append(copy)

    for i in range(min(2, groups)):
        send_pair(i)
    for i in range(groups - 1):
        send_line(i)
        if i + 2 < groups:
            send_pair(i + 2)
    total = chunk_sum(targets[-1] * 2 + core)
    pair_copies[-1].wait_recv()
    total = total + pair_in[groups - 1].astype(jnp.float32)

    for i, copy in enumerate(line_copies):
        copy.wait_recv()
        total = total + line_in[i].astype(jnp.float32)
    mixed = jnp.dot(total.astype(jnp.bfloat16), weight[...], preferred_element_type=jnp.float32) + bias[...]
    out[...] = jnp.maximum(mixed, 0.0).astype(out.dtype)

    for copy in feature_copies + pair_copies + line_copies:
        copy.wait_send()


DENSE_BYTES = 8 * 1024 * 1024


def shards(features, block_values, block_rows, block_cols, counts, weight, bias):
    wide_count = lax.axis_size("wide")
    narrow_count = lax.axis_size("narrow")
    nodes, width = features.shape
    slots, block = block_values.shape[2], block_values.shape[3]
    per_device = nodes // block
    groups = wide_count // 2
    hidden = weight.shape[1]
    tile_rows = wide_count * per_device
    panel_blocks = narrow_count * per_device
    dense_fits = tile_rows * panel_blocks * block * block * 2 <= DENSE_BYTES
    keys = tile_rows * panel_blocks if dense_fits else tile_rows
    lanes = -(-max(slots, keys) // 128) * 128
    chunks = max(c for c in (1, 2, 4) if slots % c == 0)
    others = max(narrow_count - 1, 1)
    in_vmem = pl.BlockSpec(memory_space=pltpu.VMEM)
    in_hbm = pl.BlockSpec(memory_space=pltpu.HBM)
    dma = pltpu.SemaphoreType.DMA
    return pl.pallas_call(
        functools.partial(dense_kernel if dense_fits else slot_kernel, wide_count, narrow_count),
        out_shape=jax.ShapeDtypeStruct((nodes, hidden), jnp.bfloat16),
        in_specs=[in_hbm, in_hbm] + [in_vmem] * 5,
        out_specs=in_vmem,
        scratch_shapes=[
            *(
                [
                    pltpu.VMEM((narrow_count, nodes, width), jnp.bfloat16),
                    pltpu.VMEM((slots, block, block), jnp.bfloat16),
                    pltpu.VMEM((slots + 1, block, block), jnp.bfloat16),
                    pltpu.VMEM((narrow_count, wide_count * nodes, nodes), jnp.bfloat16),
                    pltpu.VMEM((wide_count * nodes, width), jnp.float32),
                ]
                if dense_fits
                else [
                    pltpu.VMEM((panel_blocks, block, width), jnp.bfloat16),
                    pltpu.VMEM((slots, block, block), jnp.bfloat16),
                    pltpu.VMEM((slots, block, width), jnp.float32),
                ]
            ),
            pltpu.VMEM((8, lanes), jnp.int32),
            pltpu.SMEM((8, lanes), jnp.int32),
            pltpu.VMEM((groups, nodes, width), jnp.bfloat16 if dense_fits else jnp.float32),
            pltpu.VMEM((groups, nodes, width), jnp.bfloat16 if dense_fits else jnp.float32),
            pltpu.VMEM((max(groups - 1, 1), nodes, width), jnp.bfloat16),
            pltpu.VMEM((max(groups - 1, 1), nodes, width), jnp.bfloat16),
            dma((chunks,)),
            dma,
            dma,
            dma((others,)),
            dma((others,)),
            dma((groups,)),
            dma((groups,)),
            dma((max(groups - 1, 1),)),
            dma((max(groups - 1, 1),)),
        ],
        compiler_params=pltpu.CompilerParams(
            collective_id=0 if dense_fits else 1, has_side_effects=True, vmem_limit_bytes=56 * 1024 * 1024
        ),
        cost_estimate=pl.CostEstimate(
            flops=2 * slots * block * block * width, bytes_accessed=2 * slots * block * block, transcendentals=0
        ),
    )(
        features if dense_fits else features.reshape(per_device, block, width), block_values, block_rows, block_cols, counts,
        weight, bias.reshape(1, hidden),
    )


def solution(mesh):
    placed = (
        P(("wide", "narrow"), None),
        P("narrow", "wide", None, None, None),
        P("narrow", "wide", None),
        P("narrow", "wide", None),
        P("narrow", "wide"),
        P(),
        P(),
    )
    return jax.shard_map(
        shards, mesh=mesh, in_specs=placed, out_specs=P(("narrow", "wide"), None), check_vma=False
    )
```
